256 devices in a mesh: dp: 32 (over y, x, core), sub: 8 (over z).
Axes of the slice: x: 4, y: 4, z: 8, core: 2. Of those that a mesh axis runs over, the one named last changes fastest.
Arguments:
- tokens: bfloat16 [32768, 1024], P('dp', 'sub'), may hold values from -6 to 6
- lengths: int32 [1024, 2], P('dp'), may hold values from 1 to 24, 32 in all within a row
- dest: int32 [1024], P('dp'), may hold values from 0 to 31, as said below
- w_query: bfloat16 [1024, 1024], P(None, 'sub'), may hold values from -0.1875 to 0.1875
- w_key: bfloat16 [1024, 1024], P(None, 'sub'), may hold values from -0.1875 to 0.1875
- w_value: bfloat16 [1024, 1024], P(None, 'sub'), may hold values from -0.1875 to 0.1875
- w_out: bfloat16 [1024, 1024], P('sub'), may hold values from -0.1875 to 0.1875
- w_up: bfloat16 [1024, 8192], P(None, 'sub'), may hold values from -0.1875 to 0.1875
- w_down: bfloat16 [8192, 1024], P('sub'), may hold values from -0.0625 to 0.0625
- final_gain: float32 [1024], replicated, may hold values from 0.1 to 1.9
- projection: bfloat16 [1024, 1024], replicated, may hold values from -0.1875 to 0.1875
Outputs:
- pq_rows: float32 [16, 2048, 64], P('sub', 'dp')
- covariance: float32 [1024, 1024], P(('dp', 'sub'))
The draws below stay inside these ranges and needn't reach their ends.
Inputs may be any that keep to these rules, and one draw needn't show every extreme that they name: `dest`: every index of dp is the destination of exactly 32 blocks; the 32 blocks of one index of dp send at most 2 blocks to one destination, and exactly 2 to some. The lengths of each block sum to 32.
All inputs are finite; a program needn't handle non-finite values.
Results may differ from the reference program's by a relative error of at most 0.013.
Values may be sent and summed in bfloat16 or wider, within the bound.
No kernel may reach another device: no remote copies, remote signals or barrier semaphores. Data moves between devices by JAX's collectives and lax.ppermute only.
A program may use at most 64 MiB of HBM per device.

```python
import math
import jax
import jax.numpy as jnp
import numpy as np
from jax import lax

D = 1024
HEADS = 16
HDIM = 64
FF = 8192
SUBW = 64
BLK = 32
BROWS = 32
SENT = 2
MOSTLEN = 24
CAP = 2
NBLK = 1024
TOKENS = 32768
N_DP = 32


def draw_dest(key, part):
    key = jax.random.fold_in(key, 11)
    head_key, tail_key = jax.random.split(key)
    values = jnp.arange(N_DP, dtype=jnp.int32)
    mixed = jax.random.permutation(head_key, values)
    position = jnp.argsort(mixed).astype(jnp.int32)
    ranking = jnp.where(values == 1, -2, jnp.where(values == N_DP // 2, -1, position))
    chosen = jnp.argsort(ranking).astype(jnp.int32)[:BLK // CAP]
    pattern = jnp.repeat(chosen, CAP)
    source_keys = jax.random.split(tail_key, N_DP)

    def shuffle(single_key):
        return jax.random.permutation(single_key, pattern)
    shuffled = jax.vmap(shuffle)(source_keys)
    source = jnp.arange(N_DP, dtype=jnp.int32)[:, None]
    return ((source + shuffled) % N_DP).astype(jnp.int32).reshape(N_DP * BLK)


def block_levels(own_key, dims, shards, low, largest):
    loudness, own = 1.0, jax.random.fold_in(own_key, 6)
    for axis_at, shards_of in shards:
        steps = jnp.exp(jax.random.uniform(jax.random.fold_in(own, axis_at), (shards_of,), jnp.float32, low / len(shards), largest / len(shards)))
        loudness = loudness * jnp.repeat(steps, dims[axis_at] // shards_of).reshape([-1 if axis == axis_at else 1 for axis in range(len(dims))])
    return loudness


def split_up(count, total, bound, lean):
    loads = [(1 << 20) // math.isqrt(rank ** lean) + 1 for rank in range(2, count + 1)]
    surplus, counts = total - bound - (count - 1), [1] * (count - 1)
    while surplus > 0:
        candidates = [i for i in range(count - 1) if counts[i] < bound]
        whole, remaining = sum([loads[i] for i in candidates]), surplus
        for i in candidates:
            more = min(bound - counts[i], max(1, remaining * loads[i] // whole), surplus)
            counts[i] = counts[i] + more
            surplus = surplus - more
    return np.array([bound] + counts)


def uneven(key, number_of, total, limit, skew):
    if number_of == 2:
        one = jax.random.randint(key, (), max(1, total - limit), min(limit, total - 1) + 1)
        return jnp.stack([one, total - one])
    tallies = jnp.asarray(split_up(number_of, total, limit, skew), jnp.int32)
    pairs = (number_of - 1) // 2
    donor, receiver = tallies[1:1 + 2 * pairs:2], tallies[2:2 + 2 * pairs:2]
    slack = jnp.minimum(donor - 1, limit - receiver)
    passed = jax.random.randint(jax.random.fold_in(key, 1), (pairs,), 0, 1 << 20) % (slack + 1)
    tallies = tallies.at[1:1 + 2 * pairs:2].set(donor - passed).at[2:2 + 2 * pairs:2].set(receiver + passed)
    return tallies[jax.random.permutation(jax.random.fold_in(key, 2), number_of)]


def bell_draw(own_key, shape, scale, most, cuts=(), kind=jnp.bfloat16):
    entries = jax.random.normal(own_key, shape, jnp.float32) * scale
    if len(cuts) > 0:
        entries = block_levels(own_key, shape, cuts, -0.22, 0.18) * entries
    return jnp.clip(entries, min=-most, max=most).astype(kind)


def setup_inputs(seed: int = 0) -> dict:
    keys = jax.random.split(jax.random.key(seed), 12)
    return {
        "tokens": bell_draw(keys[0], (TOKENS, D), 1.0, 6.0, ((0, 32), (1, 8))),
        "lengths": jax.vmap(lambda own: uneven(own, SENT, BROWS, MOSTLEN, 2))(jax.random.split(keys[1], NBLK)).reshape((NBLK, SENT)).astype(jnp.int32),
        "dest": draw_dest(jax.random.fold_in(keys[11], 71), 0),
        "w_query": bell_draw(keys[3], (D, D), D ** -0.5, 0.1875, ((1, 8),)),
        "w_key": bell_draw(keys[4], (D, D), D ** -0.5, 0.1875, ((1, 8),)),
        "w_value": bell_draw(keys[5], (D, D), D ** -0.5, 0.1875, ((1, 8),)),
        "w_out": bell_draw(keys[6], (D, D), D ** -0.5, 0.1875, ((0, 8),)),
        "w_up": bell_draw(keys[7], (D, FF), D ** -0.5, 0.1875, ((1, 8),)),
        "w_down": bell_draw(keys[8], (FF, D), FF ** -0.5, 0.0625, ((0, 8),)),
        "final_gain": jnp.clip(1.0 + 0.18 * jax.random.normal(keys[9], (D,), jnp.float32), 0.1, 1.9),
        "projection": bell_draw(keys[10], (D, D), D ** -0.5, 0.1875),
    }


epsilon = 1e-05

def normalize(rows):
    center = lax.optimization_barrier(jnp.mean(rows, axis=-1, keepdims=True))
    shifted = rows - center
    spread = lax.optimization_barrier(jnp.mean(shifted * shifted, axis=-1, keepdims=True))
    return shifted / jnp.sqrt(spread + epsilon)

def segment_ids(block_lens, block_rows):
    ends = jnp.cumsum(block_lens, axis=-1)
    position = jnp.arange(block_rows, dtype=jnp.int32)
    return lax.optimization_barrier(jnp.sum((ends[:, None, :] <= position[None, :, None]).astype(jnp.int32), axis=-1))

def attend(query_rows, key_rows, value_rows, segment):
    scores = jnp.einsum('bqhd,bkhd->bhqk', query_rows.astype(jnp.float32), key_rows.astype(jnp.float32)) / math.sqrt(HDIM)
    matches = segment[:, None, :, None] == segment[:, None, None, :]
    raised = jnp.where(matches, jnp.exp(scores), 0.0)
    weights = (raised / lax.optimization_barrier(jnp.sum(raised, axis=-1, keepdims=True))).astype(jnp.bfloat16)
    context = jnp.einsum('bhqk,bkhd->bqhd', weights.astype(jnp.float32), value_rows.astype(jnp.float32))
    return context.astype(jnp.bfloat16)

def reference(tokens, lengths, dest, w_query, w_key, w_value, w_out, w_up, w_down, final_gain, projection):
    block_total = lengths.shape[0]
    width = tokens.shape[1]
    index = jnp.arange(block_total, dtype=jnp.int32)
    order = jnp.argsort(dest.astype(jnp.int32) * block_total + index).astype(jnp.int32)
    blocks = tokens.reshape(block_total, BROWS, width)[order]
    block_lens = lengths[order]
    groups = block_total // BLK
    blocks = blocks.reshape(groups, BLK, BROWS, width)
    block_lens = block_lens.reshape(groups, BLK, SENT)

    def layer(inputs):
        group_rows, group_lens = inputs
        segment = segment_ids(group_lens, BROWS)
        residual = group_rows.reshape(BLK * BROWS, width).astype(jnp.float32)
        normed = normalize(residual).astype(jnp.bfloat16)
        shape4 = (BLK, BROWS, HEADS, HDIM)
        query_rows = jnp.dot(normed, w_query, preferred_element_type=jnp.float32).astype(jnp.bfloat16).reshape(shape4)
        key_rows = jnp.dot(normed, w_key, preferred_element_type=jnp.float32).astype(jnp.bfloat16).reshape(shape4)
        value_rows = jnp.dot(normed, w_value, preferred_element_type=jnp.float32).astype(jnp.bfloat16).reshape(shape4)
        context = attend(query_rows, key_rows, value_rows, segment).reshape(BLK * BROWS, width)
        hidden1 = residual + jnp.dot(context, w_out, preferred_element_type=jnp.float32)
        normed2 = normalize(hidden1).astype(jnp.bfloat16)
        inner = jnp.maximum(jnp.dot(normed2, w_up, preferred_element_type=jnp.float32), 0.0).astype(jnp.bfloat16)
        hidden2 = hidden1 + jnp.dot(inner, w_down, preferred_element_type=jnp.float32)
        finished = normalize(hidden2) * final_gain
        onehot = (segment[..., None] == jnp.arange(SENT, dtype=jnp.int32)).astype(jnp.float32)
        totals = jnp.einsum('brs,brd->bsd', onehot, finished.reshape(BLK, BROWS, width), precision=lax.Precision.HIGHEST)
        pooled = totals / group_lens[..., None].astype(jnp.float32)
        return pooled.reshape(BLK * SENT, width)
    pooled = lax.map(layer, (blocks, block_lens)).reshape(groups * BLK * SENT, width)
    sentence_total = pooled.shape[0]
    column_mean = lax.optimization_barrier(jnp.sum(pooled, axis=0)) / sentence_total
    centred = pooled - column_mean
    covariance = jnp.dot(centred.T, centred, precision=lax.Precision.HIGHEST) / sentence_total
    rounded = centred.astype(jnp.bfloat16)
    rotated = jnp.dot(rounded, projection, preferred_element_type=jnp.float32)
    pq_rows = rotated.reshape(sentence_total, width // SUBW, SUBW).transpose(1, 0, 2)
    return (pq_rows, covariance)
```

```python
import functools
import math

import jax
import jax.numpy as jnp
from jax import lax
from jax.experimental import pallas as pl
from jax.experimental.pallas import tpu as pltpu
from jax.sharding import PartitionSpec as P

HDIM = 64
SUBW = 64
LANES = 128
SLOTS = 2

epsilon = 1e-05
BF = jnp.bfloat16
F32 = jnp.float32
HIGH = lax.Precision.HIGHEST


def normalize(rows):
    center = jnp.mean(rows, axis=-1, keepdims=True)
    shifted = rows - center
    spread = jnp.mean(shifted * shifted, axis=-1, keepdims=True)
    return shifted * lax.rsqrt(spread + epsilon)


def dot(a, b, dims=((1,), (0,)), precision=None):
    return lax.dot_general(a, b, (dims, ((), ())), precision=precision, preferred_element_type=F32)


def attention_kernel(x_ref, wq_ref, wk_ref, wv_ref, wo_ref, row_ref, col_ref, out_ref):
    rows = jnp.concatenate([x_ref[k] for k in range(x_ref.shape[0])], axis=-1).astype(F32)
    normed = normalize(rows).astype(BF)
    query = dot(normed, wq_ref[...]).astype(BF)
    key = dot(normed, wk_ref[...]).astype(BF)
    value = dot(normed, wv_ref[...]).astype(BF)
    matches = row_ref[...] == col_ref[...]
    heads = []
    for h in range(query.shape[1] // HDIM):
        cut = slice(h * HDIM, (h + 1) * HDIM)
        scores = dot(query[:, cut], key[:, cut], ((1,), (1,))) / math.sqrt(HDIM)
        raised = jnp.where(matches, jnp.exp(scores), 0.0)
        weights = (raised / jnp.sum(raised, axis=-1, keepdims=True)).astype(BF)
        heads.append(dot(weights, value[:, cut]).astype(BF))
    context = jnp.concatenate(heads, axis=-1)
    out_ref[...] = dot(context, wo_ref[...]).astype(BF)


def attention(gathered, w_query, w_key, w_value, w_out, keys):
    parts, rows, part = gathered.shape
    chunk = 128
    width = w_out.shape[1]
    whole = lambda a: pl.BlockSpec(a.shape, lambda i: (0,) * a.ndim)
    return pl.pallas_call(
        attention_kernel,
        grid=(rows // chunk,),
        in_specs=[
            pl.BlockSpec((parts, chunk, part), lambda i: (0, i, 0)),
            whole(w_query),
            whole(w_key),
            whole(w_value),
            whole(w_out),
            pl.BlockSpec((chunk, 1), lambda i: (i, 0)),
            pl.BlockSpec((1, chunk), lambda i: (0, i)),
        ],
        out_specs=pl.BlockSpec((chunk, width), lambda i: (i, 0)),
        out_shape=jax.ShapeDtypeStruct((rows, width), BF),
        compiler_params=pltpu.CompilerParams(vmem_limit_bytes=32 << 20),
        name="attention",
    )(gathered, w_query, w_key, w_value, w_out, keys[:, None], keys[None, :])


def pool_kernel(hidden_ref, gain_ref, member_ref, length_ref, out_ref):
    finished = normalize(hidden_ref[...]) * gain_ref[...]
    out_ref[...] = dot(member_ref[...], finished, precision=HIGH) / length_ref[...]


def moments_kernel(sub_ref, pooled_ref, proj_ref, code_ref, out_ref):
    me = sub_ref[0]
    pooled = pooled_ref[...]
    sentences, width = pooled.shape
    groups = out_ref.shape[0]
    per_group = width // groups
    own = out_ref.shape[1] // width - 3
    mean = jnp.mean(pooled, axis=0, keepdims=True)
    centred = pooled - mean
    feature = lax.broadcasted_iota(jnp.int32, (width, own * groups), 0)
    wanted = lax.broadcasted_iota(jnp.int32, (width, own * groups), 1)
    chosen = (wanted % groups) * per_group + me * own + wanted // groups
    pick = (feature == chosen).astype(F32)
    picked = dot(centred, pick, precision=HIGH)
    moments = dot(picked, centred, ((0,), (0,)), precision=HIGH)
    for j in range(own):
        out_ref[:, j * width:(j + 1) * width] = moments[j * groups:(j + 1) * groups].astype(BF)
    high = mean.astype(BF)
    low = (mean - high.astype(F32)).astype(BF)
    out_ref[:, own * width:(own + 1) * width] = jnp.broadcast_to(high, (groups, width))
    out_ref[:, (own + 1) * width:(own + 2) * width] = jnp.broadcast_to(low, (groups, width))
    rotated = dot(centred.astype(BF), proj_ref[...]).astype(BF)
    lanes = rotated.shape[1]
    kinds = 4
    target = lax.broadcasted_iota(jnp.int32, (kinds * groups, sentences), 0)
    target = (target % groups) * kinds + target // groups
    place = (target == code_ref[...]).astype(BF)
    placed = dot(place, rotated).astype(BF)
    filled = dot(place, jnp.ones((sentences, lanes), BF)).astype(BF)
    start = (own + 2) * width
    for k in range(kinds):
        out_ref[:, start + k * lanes:start + (k + 1) * lanes] = placed[k * groups:(k + 1) * groups]
        out_ref[:, start + (kinds + k) * lanes:start + (kinds + k + 1) * lanes] = filled[k * groups:(k + 1) * groups]


def combine_kernel(where_ref, recv_ref, proj_ref, pq_ref, cov_ref):
    first = where_ref[0]
    groups = recv_ref.shape[0]
    own, width = cov_ref.shape
    sentences = pq_ref.shape[1]
    total = float(groups * sentences)
    high = recv_ref[:, own * width:(own + 1) * width].astype(F32)
    low = recv_ref[:, (own + 1) * width:(own + 2) * width].astype(F32)
    means = high + low
    away = means - jnp.mean(means, axis=0, keepdims=True)
    feature = lax.broadcasted_iota(jnp.int32, (width, LANES), 0)
    lane = lax.broadcasted_iota(jnp.int32, (width, LANES), 1)
    pick = ((feature == first + lane) & (lane < own)).astype(F32)
    picked = dot(away, pick, precision=HIGH)
    between = dot(picked, away, ((0,), (0,)), precision=HIGH)
    for j in range(own):
        within = jnp.sum(recv_ref[:, j * width:(j + 1) * width].astype(F32), axis=0, keepdims=True)
        cov_ref[j:j + 1, :] = (within + float(sentences) * between[j:j + 1]) / total
    shift = dot(away, proj_ref[...].astype(F32), precision=HIGH)
    lanes = shift.shape[1]
    start = (own + 2) * width
    kinds = 4
    source = lax.broadcasted_iota(jnp.int32, (groups, groups), 0)
    other = lax.broadcasted_iota(jnp.int32, (groups, groups), 1)
    ahead = (source < other).astype(BF)
    same = (source == other).astype(BF)
    flags = [
        recv_ref[:, start + (kinds + 2 * c) * lanes:start + (kinds + 2 * c + 1) * lanes] for c in range(SLOTS)
    ]
    flat = [dot(f[:, :8], same, ((0,), (0,)))[:1] for f in flags]
    before = dot((flags[0] + flags[1])[:, :8], ahead, ((0,), (0,)))[:1]
    place = lax.broadcasted_iota(jnp.int32, (sentences, groups), 0)
    result = jnp.zeros((sentences, lanes), F32)
    for c in range(SLOTS):
        for k in range(2):
            rows = recv_ref[:, start + (2 * c + k) * lanes:start + (2 * c + k + 1) * lanes].astype(F32) + shift
            position = (2.0 * before + float(k)).astype(jnp.int32)
            chosen = jnp.where((place == position) & (flat[c] > 0.5), 1.0, 0.0)
            result = result + dot(chosen, rows, precision=HIGH)
        before = before + flat[c]
    for q in range(pq_ref.shape[0]):
        pq_ref[q] = result[:, q * SUBW:(q + 1) * SUBW]


def small_call(kernel, outs, args, scalar=None, name=None):
    specs = [pl.BlockSpec(memory_space=pltpu.VMEM) for _ in args]
    if scalar is not None:
        specs = [pl.BlockSpec(memory_space=pltpu.SMEM)] + specs
        args = (scalar,) + tuple(args)
    single = not isinstance(outs, (tuple, list))
    return pl.pallas_call(
        kernel,
        in_specs=specs,
        out_specs=pl.BlockSpec(memory_space=pltpu.VMEM) if single else [pl.BlockSpec(memory_space=pltpu.VMEM) for _ in outs],
        out_shape=outs,
        compiler_params=pltpu.CompilerParams(vmem_limit_bytes=32 << 20),
        name=name,
    )(*args)


def on_device(
    tokens, lengths, dest, w_query, w_key, w_value, w_out, w_up, w_down, final_gain, projection
):
    dp_count = lax.axis_size("dp")
    sub_count = lax.axis_size("sub")
    dp_at = lax.axis_index("dp")
    sub_at = lax.axis_index("sub")
    block_count, per_block = lengths.shape
    local_rows, local_width = tokens.shape
    block_rows = local_rows // block_count
    width = local_width * sub_count
    own_blocks = block_count // sub_count
    own_rows = own_blocks * block_rows

    ends = jnp.cumsum(lengths, axis=-1)
    position = jnp.arange(block_rows, dtype=jnp.int32)
    segment = jnp.sum((ends[:, None, :] <= position[None, :, None]).astype(jnp.int32), axis=-1)
    ordinal = jnp.arange(block_count, dtype=jnp.int32)
    keys = (ordinal[:, None] * per_block + segment).reshape(local_rows)
    own_lens = lax.dynamic_slice_in_dim(lengths, sub_at * own_blocks, own_blocks, 0)
    own_keys = lax.dynamic_slice_in_dim(keys, sub_at * own_rows, own_rows, 0)
    own_sentences = own_blocks * per_block
    member = (
        own_keys[None, :] == sub_at * own_sentences + jnp.arange(own_sentences, dtype=jnp.int32)[:, None]
    ).astype(F32)
    matches = dest[:, None] == dest[None, :]
    earlier = ordinal[:, None] > ordinal[None, :]
    earlier_count = jnp.sum((matches & earlier).astype(jnp.int32), axis=1)
    code = (dest * SLOTS + earlier_count)[:, None] * per_block + jnp.arange(per_block, dtype=jnp.int32)[None, :]
    code = code.reshape(1, block_count * per_block)

    gathered = lax.all_gather(tokens, "sub", axis=0, tiled=False)
    residual = lax.dynamic_slice_in_dim(gathered, sub_at * own_rows, own_rows, 1)
    residual = residual.transpose(1, 0, 2).reshape(own_rows, width).astype(F32)
    attended = attention(gathered, w_query, w_key, w_value, w_out, keys)
    hidden1 = residual + lax.psum_scatter(attended, "sub", scatter_dimension=0, tiled=True).astype(F32)
    normed2 = normalize(hidden1).astype(BF)
    inner = jnp.maximum(
        jnp.dot(lax.all_gather(normed2, "sub", axis=0, tiled=True), w_up, preferred_element_type=F32), 0.0
    ).astype(BF)
    hidden2 = hidden1 + lax.psum_scatter(
        jnp.dot(inner, w_down, preferred_element_type=F32).astype(BF), "sub", scatter_dimension=0, tiled=True
    ).astype(F32)
    pooled = small_call(
        pool_kernel,
        jax.ShapeDtypeStruct((own_sentences, width), F32),
        (hidden2, final_gain[None, :], member, own_lens.reshape(own_sentences, 1).astype(F32)),
        name="pool",
    )
    pooled = lax.all_to_all(
        jnp.broadcast_to(pooled[None], (sub_count, own_sentences, width)),
        "sub", split_axis=0, concat_axis=0, tiled=True,
    ).reshape(sub_count * own_sentences, width)
    sentences = sub_count * own_sentences
    cov_rows = width // (dp_count * sub_count)
    columns = width // sub_count
    proj = lax.dynamic_slice_in_dim(projection, sub_at * columns, columns, 1)
    sent = small_call(
        moments_kernel,
        jax.ShapeDtypeStruct((dp_count, (cov_rows + 3) * width), BF),
        (pooled, proj, code),
        scalar=sub_at.reshape(1),
        name="moments",
    )
    received = lax.all_to_all(sent, "dp", split_axis=0, concat_axis=0, tiled=True)
    return small_call(
        combine_kernel,
        (
            jax.ShapeDtypeStruct((columns // SUBW, sentences, SUBW), F32),
            jax.ShapeDtypeStruct((cov_rows, width), F32),
        ),
        (received, proj),
        scalar=((dp_at * sub_count + sub_at) * cov_rows).reshape(1),
        name="combine",
    )


def solution(mesh):
    in_specs = (
        P("dp", "sub"),
        P("dp", None),
        P("dp"),
        P(None, "sub"),
        P(None, "sub"),
        P(None, "sub"),
        P("sub", None),
        P(None, "sub"),
        P("sub", None),
        P(),
        P(),
    )
    out_specs = (P("sub", "dp", None), P(("dp", "sub"), None))
    return jax.shard_map(
        on_device, mesh=mesh, in_specs=in_specs, out_specs=out_specs, check_vma=False
    )
```

```python
import functools
import math

import jax
import jax.numpy as jnp
from jax import lax
from jax.experimental import pallas as pl
from jax.experimental.pallas import tpu as pltpu
from jax.sharding import PartitionSpec as P

HDIM = 64
SUBW = 64
LANES = 128
SLOTS = 2
KINDS = 4
PACK = 8

epsilon = 1e-05
BF = jnp.bfloat16
F32 = jnp.float32
HIGH = lax.Precision.HIGHEST
VMEM_LIMIT = 48 << 20


def normalize(rows):
    center = jnp.mean(rows, axis=-1, keepdims=True)
    shifted = rows - center
    spread = jnp.mean(shifted * shifted, axis=-1, keepdims=True)
    return shifted * lax.rsqrt(spread + epsilon)


def dot(a, b, dims=((1,), (0,)), precision=None):
    return lax.dot_general(a, b, (dims, ((), ())), precision=precision, preferred_element_type=F32)


def cost(flops, size):
    return pl.CostEstimate(flops=flops, bytes_accessed=size, transcendentals=0)


def attention_kernel(parts, order_ref, *refs):
    pieces, (w_ref, wo_ref, row_ref, col_ref), outs = refs[:parts], refs[parts:parts + 4], refs[parts + 4:]
    rows_ref = outs[-1]
    me = order_ref[0]
    half = parts // 2
    part = pieces[0].shape[1]
    for k in range(parts):
        at = lax.rem(me + (k if k <= half else parts - (k - half)), parts)
        rows_ref[:, pl.ds(pl.multiple_of(at * part, part), part)] = pieces[k][...]
    rows = rows_ref[...].astype(F32)
    if len(outs) > 2:
        outs[1][...] = rows
    normed = normalize(rows).astype(BF)
    projected = dot(normed, w_ref[...]).astype(BF)
    local = wo_ref.shape[0]
    matches = row_ref[...] == col_ref[...]
    heads = []
    for h in range(local // HDIM):
        query, key, value = (
            projected[:, t * local + h * HDIM:t * local + (h + 1) * HDIM] for t in range(3)
        )
        scores = dot(query, key, ((1,), (1,))) / math.sqrt(HDIM)
        raised = jnp.where(matches, jnp.exp(scores), 0.0)
        weights = (raised / jnp.sum(raised, axis=-1, keepdims=True)).astype(BF)
        heads.append(dot(weights, value).astype(BF))
    context = jnp.concatenate(heads, axis=-1)
    outs[0][...] = dot(context, wo_ref[...])


def attention(pieces, w_qkv, w_out, keys, me, chunks, chunk, with_rows=False):
    parts = len(pieces)
    part = pieces[0].shape[1]
    width = w_out.shape[1]
    count = len(chunks)
    order = jnp.stack([me] + [lax.rem(me + c + parts, parts) for c in chunks]).astype(jnp.int32)
    whole = lambda a: pl.BlockSpec(a.shape, lambda i, o: (0,) * a.ndim)
    outs = [jax.ShapeDtypeStruct((count * chunk, width), F32)]
    if with_rows:
        outs.append(jax.ShapeDtypeStruct((count * chunk, width), F32))
    result = pl.pallas_call(
        functools.partial(attention_kernel, parts),
        grid_spec=pltpu.PrefetchScalarGridSpec(
            num_scalar_prefetch=1,
            grid=(count,),
            in_specs=[pl.BlockSpec((chunk, part), lambda i, o: (o[1 + i], 0)) for _ in range(parts)]
            + [
                whole(w_qkv),
                whole(w_out),
                pl.BlockSpec((chunk, 1), lambda i, o: (o[1 + i], 0)),
                pl.BlockSpec((1, chunk), lambda i, o: (0, o[1 + i])),
            ],
            out_specs=[pl.BlockSpec((chunk, width), lambda i, o: (i, 0)) for _ in outs],
            scratch_shapes=[pltpu.VMEM((chunk, width), BF)],
        ),
        out_shape=outs,
        compiler_params=pltpu.CompilerParams(vmem_limit_bytes=VMEM_LIMIT),
        cost_estimate=cost(count * 2 * chunk * width * 4 * w_out.shape[0], 3 << 20),
        name="attention",
    )(order, *pieces, w_qkv, w_out, keys[:, None], keys[None, :])
    return result if with_rows else result[0]


def middle_kernel(rows_ref, own_ref, right_ref, left_ref, hidden_ref, normed_ref):
    hidden = rows_ref[...] + (own_ref[...] + right_ref[...].astype(F32) + left_ref[...].astype(F32))
    hidden_ref[...] = hidden
    normed_ref[...] = normalize(hidden).astype(BF)


def feed_kernel(cuts, own_ref, pair_ref, up_ref, down_ref, gup_ref, gdown_ref, out_ref, send_ref, acc_ref):
    step = pl.program_id(0)
    count = own_ref.shape[0]
    rows = jnp.concatenate([own_ref[...], pair_ref[...]], axis=0)

    def add(up, down):
        inner = jnp.maximum(dot(rows, up), 0.0).astype(BF)
        return dot(inner, down)

    @pl.when(step == 0)
    def _():
        acc_ref[...] = jnp.zeros_like(acc_ref)

    @pl.when(step < cuts)
    def _():
        acc_ref[...] += add(up_ref[...], down_ref[...])

    @pl.when(step >= cuts)
    def _():
        up = gup_ref[...].reshape(-1, gup_ref.shape[-1])
        down = gdown_ref[...].reshape(-1, gdown_ref.shape[-1])
        acc_ref[...] += add(up, down)

    @pl.when(step == pl.num_programs(0) - 1)
    def _():
        out_ref[...] = acc_ref[:count]
        send_ref[...] = acc_ref[count:].astype(BF)


def feed(own, pair, w_up, w_down, gathered):
    spread, planes, both, width = gathered.shape
    rows = both // 2
    count = own.shape[0]
    hidden = w_up.shape[1]
    cuts = 2
    cut = hidden // cuts
    whole = lambda a: pl.BlockSpec(a.shape, lambda i: (0,) * a.ndim)
    late = lambda i: jnp.maximum(i - cuts, 0)
    early = lambda i: jnp.minimum(i, cuts - 1)
    return pl.pallas_call(
        functools.partial(feed_kernel, cuts),
        grid=(cuts * (planes + 1),),
        in_specs=[
            whole(own),
            whole(pair),
            pl.BlockSpec((width, cut), lambda i: (0, early(i))),
            pl.BlockSpec((cut, width), lambda i: (early(i), 0)),
            pl.BlockSpec((spread, 1, rows, cut), lambda i: (0, late(i) // cuts, 0, late(i) % cuts)),
            pl.BlockSpec((spread // cuts, 1, rows, width), lambda i: (late(i) % cuts, late(i) // cuts, 1, 0)),
        ],
        out_specs=[whole(own), whole(own)],
        out_shape=[jax.ShapeDtypeStruct(own.shape, F32), jax.ShapeDtypeStruct(own.shape, BF)],
        scratch_shapes=[pltpu.VMEM((2 * count, width), F32)],
        compiler_params=pltpu.CompilerParams(vmem_limit_bytes=VMEM_LIMIT),
        cost_estimate=cost(8 * count * width * hidden * (planes + 1), 4 * (planes + 1) * width * hidden),
        name="feed",
    )(own, pair, w_up, w_down, gathered, gathered)


def pool_kernel(hidden_ref, own_ref, pair_ref, gain_ref, member_ref, length_ref, out_ref):
    hidden = hidden_ref[...] + (own_ref[...] + pair_ref[...].astype(F32))
    finished = normalize(hidden) * gain_ref[...]
    pooled = dot(member_ref[...], finished, precision=HIGH) / length_ref[...]
    out_ref[...] = jnp.broadcast_to(pooled[None], out_ref.shape)


def moments_kernel(sub_ref, pooled_ref, proj_ref, code_ref, out_ref):
    me = sub_ref[0]
    parts, few, width = pooled_ref.shape
    sentences = parts * few
    pooled = pooled_ref[...].reshape(sentences, width)
    total = out_ref.shape[0]
    groups = total // PACK
    per_group = width // groups
    own = per_group // parts
    mean = jnp.mean(pooled, axis=0, keepdims=True)
    centred = pooled - mean
    feature = lax.broadcasted_iota(jnp.int32, (width, total), 0)
    wanted = lax.broadcasted_iota(jnp.int32, (width, total), 1)
    chosen = (wanted // PACK) * per_group + me * own + wanted % PACK
    pick = jnp.where((feature == chosen) & (wanted % PACK < own), 1.0, 0.0)
    picked = dot(centred, pick, precision=HIGH)
    moments = dot(picked, centred, ((0,), (0,)), precision=HIGH)
    rotated = dot(centred.astype(BF), proj_ref[...]).astype(BF)
    lanes = rotated.shape[1]
    row = lax.broadcasted_iota(jnp.int32, (total, sentences), 0)
    pieces = []
    flags = []
    ones = jnp.ones((sentences, lanes), BF)
    for k in range(KINDS):
        place = (row % PACK == own + 2) & ((row // PACK) * KINDS + k == code_ref[...])
        place = jnp.where(place, 1.0, 0.0).astype(BF)
        pieces.append(dot(place, rotated))
        flags.append(dot(place, ones))
    sides = jnp.concatenate(pieces + flags, axis=-1)
    high = mean.astype(BF).astype(F32)
    low = mean - high
    line = lax.broadcasted_iota(jnp.int32, (total, 1), 0) % PACK
    means = jnp.where(line == own, high, 0.0) + jnp.where(line == own + 1, low, 0.0)
    out_ref[...] = (moments + means + sides).astype(BF)


def combine_kernel(where_ref, recv_ref, proj_ref, pq_ref, cov_ref):
    first = where_ref[0]
    own, width = cov_ref.shape
    recv = recv_ref[...]
    total = recv.shape[0]
    groups = total // PACK
    sentences = pq_ref.shape[1]
    count = float(groups * sentences)
    source = lax.broadcasted_iota(jnp.int32, (groups, total), 0)
    line = lax.broadcasted_iota(jnp.int32, (groups, total), 1)
    pick_mean = (line == source * PACK + own) | (line == source * PACK + own + 1)
    means = dot(jnp.where(pick_mean, 1.0, 0.0).astype(BF), recv)
    sides = dot(jnp.where(line == source * PACK + own + 2, 1.0, 0.0).astype(BF), recv)
    line = lax.broadcasted_iota(jnp.int32, (PACK, total), 1) % PACK
    within = dot(jnp.where(line == lax.broadcasted_iota(jnp.int32, (PACK, total), 0), 1.0, 0.0).astype(BF), recv)
    away = means - jnp.mean(means, axis=0, keepdims=True)
    feature = lax.broadcasted_iota(jnp.int32, (width, LANES), 0)
    lane = lax.broadcasted_iota(jnp.int32, (width, LANES), 1)
    pick = jnp.where((feature == first + lane) & (lane < own), 1.0, 0.0)
    picked = dot(away, pick, precision=HIGH)
    between = dot(picked, away, ((0,), (0,)), precision=HIGH)
    cov_ref[...] = (within[:own] + float(sentences) * between[:own]) / count
    shift = dot(away, proj_ref[...].astype(F32), precision=HIGH)
    lanes = shift.shape[1]
    one = lax.broadcasted_iota(jnp.int32, (groups, groups), 0)
    other = lax.broadcasted_iota(jnp.int32, (groups, groups), 1)
    ahead = jnp.where(one < other, 1.0, 0.0).astype(BF)
    same = jnp.where(one == other, 1.0, 0.0).astype(BF)
    filled = [sides[:, (KINDS + 2 * c) * lanes:(KINDS + 2 * c + 1) * lanes] for c in range(SLOTS)]
    flat = [dot(f.astype(BF), same, ((0,), (0,)))[:1] for f in filled]
    before = dot((filled[0] + filled[1]).astype(BF), ahead, ((0,), (0,)))[:1]
    place = lax.broadcasted_iota(jnp.int32, (sentences, groups), 0)
    result = jnp.zeros((sentences, lanes), F32)
    for c in range(SLOTS):
        for k in range(2):
            rows = sides[:, (2 * c + k) * lanes:(2 * c + k + 1) * lanes] + shift
            position = (2.0 * before + float(k)).astype(jnp.int32)
            chosen = jnp.where((place == position) & (flat[c] > 0.5), 1.0, 0.0)
            result = result + dot(chosen, rows, precision=HIGH)
        before = before + flat[c]
    for q in range(pq_ref.shape[0]):
        pq_ref[q] = result[:, q * SUBW:(q + 1) * SUBW]


def small_call(kernel, outs, args, scalar=None, name=None):
    specs = [pl.BlockSpec(memory_space=pltpu.VMEM) for _ in args]
    if scalar is not None:
        specs = [pl.BlockSpec(memory_space=pltpu.SMEM)] + specs
        args = (scalar,) + tuple(args)
    single = not isinstance(outs, (tuple, list))
    return pl.pallas_call(
        kernel,
        in_specs=specs,
        out_specs=pl.BlockSpec(memory_space=pltpu.VMEM) if single else [pl.BlockSpec(memory_space=pltpu.VMEM) for _ in outs],
        out_shape=outs,
        compiler_params=pltpu.CompilerParams(vmem_limit_bytes=32 << 20),
        cost_estimate=cost(1 << 20, 1 << 20),
        name=name,
    )(*args)


def on_device(
    tokens, lengths, dest, w_query, w_key, w_value, w_out, w_up, w_down, final_gain, projection
):
    dp_count = lax.axis_size("dp")
    sub_count = lax.axis_size("sub")
    dp_at = lax.axis_index("dp")
    sub_at = lax.axis_index("sub")
    block_count, per_block = lengths.shape
    local_rows, local_width = tokens.shape
    block_rows = local_rows // block_count
    width = local_width * sub_count
    own_blocks = block_count // sub_count
    own_rows = own_blocks * block_rows
    half = sub_count // 2

    def move(array, by):
        return lax.ppermute(array, "sub", [(i, (i + by) % sub_count) for i in range(sub_count)])

    def swap(array):
        return lax.ppermute(array, "sub", [(i, i ^ 1) for i in range(sub_count)])

    rows = w_up.shape[0] // dp_count
    piece = jnp.concatenate(
        [lax.dynamic_slice_in_dim(w, dp_at * rows, rows, 0) for w in (w_up, w_down)], axis=0
    )
    others = jnp.concatenate([move(piece, by) for by in range(2, sub_count, 2)], axis=0)
    planes = half - 1

    ends = jnp.cumsum(lengths, axis=-1)
    position = jnp.arange(block_rows, dtype=jnp.int32)
    segment = jnp.sum((ends[:, None, :] <= position[None, :, None]).astype(jnp.int32), axis=-1)
    ordinal = jnp.arange(block_count, dtype=jnp.int32)
    keys = (ordinal[:, None] * per_block + segment).reshape(local_rows)
    own_lens = lax.dynamic_slice_in_dim(lengths, sub_at * own_blocks, own_blocks, 0)
    own_keys = lax.dynamic_slice_in_dim(keys, sub_at * own_rows, own_rows, 0)
    own_sentences = own_blocks * per_block
    member = (
        own_keys[None, :] == sub_at * own_sentences + jnp.arange(own_sentences, dtype=jnp.int32)[:, None]
    ).astype(F32)
    matches = dest[:, None] == dest[None, :]
    earlier = ordinal[:, None] > ordinal[None, :]
    earlier_count = jnp.sum((matches & earlier).astype(jnp.int32), axis=1)
    code = (dest * SLOTS + earlier_count)[:, None] * per_block + jnp.arange(per_block, dtype=jnp.int32)[None, :]
    code = code.reshape(1, block_count * per_block)
    w_qkv = jnp.concatenate((w_query, w_key, w_value), axis=1)
    columns = width // sub_count
    proj = lax.dynamic_slice_in_dim(projection, sub_at * columns, columns, 1)

    behind, before = [], []
    right = left = tokens
    for _ in range(half - 1):
        right, left = move(right, 1), move(left, -1)
        behind.append(right)
        before.append(left)
    middle = local_rows // 2
    far = jnp.concatenate([move(right[:middle], 1), move(left[middle:], -1)], axis=0)
    pieces = [tokens] + before + [far] + behind

    gathered = lax.all_gather(others, "dp", axis=0, tiled=True).reshape(dp_count, planes, 2 * rows, width)

    attend = functools.partial(attention, pieces, w_qkv, w_out, keys, sub_at, chunk=own_rows)
    part = attend(chunks=[half]).astype(BF)
    right, left = move(part[:own_rows // 2], 1), move(part[own_rows // 2:], -1)
    for away in range(half - 1, 0, -1):
        part = attend(chunks=[away, -away])
        ahead, back = part[:own_rows], part[own_rows:]
        if away == half - 1:
            right = jnp.concatenate([ahead[:own_rows // 2] + right.astype(F32), ahead[own_rows // 2:]], axis=0)
            left = jnp.concatenate([back[:own_rows // 2], back[own_rows // 2:] + left.astype(F32)], axis=0)
        else:
            right = ahead + right.astype(F32)
            left = back + left.astype(F32)
        right, left = move(right.astype(BF), 1), move(left.astype(BF), -1)
    part, residual = attend(chunks=[0], with_rows=True)
    own_shape = (own_rows, width)
    hidden1, normed2 = small_call(
        middle_kernel,
        (jax.ShapeDtypeStruct(own_shape, F32), jax.ShapeDtypeStruct(own_shape, BF)),
        (residual, part, right, left),
        name="middle",
    )
    fed, sent = feed(normed2, swap(normed2), w_up, w_down, gathered)
    pooled = small_call(
        pool_kernel,
        jax.ShapeDtypeStruct((sub_count, own_sentences, width), F32),
        (hidden1, fed, swap(sent), final_gain[None, :], member, own_lens.reshape(own_sentences, 1).astype(F32)),
        name="pool",
    )
    pooled = lax.all_to_all(pooled, "sub", split_axis=0, concat_axis=0, tiled=True)
    sentences = sub_count * own_sentences
    cov_rows = width // (dp_count * sub_count)
    sent = small_call(
        moments_kernel,
        jax.ShapeDtypeStruct((dp_count * PACK, width), BF),
        (pooled, proj, code),
        scalar=sub_at.reshape(1),
        name="moments",
    )
    received = lax.all_to_all(
        sent.reshape(dp_count, PACK, width), "dp", split_axis=0, concat_axis=0, tiled=True
    ).reshape(dp_count * PACK, width)
    return small_call(
        combine_kernel,
        (
            jax.ShapeDtypeStruct((columns // SUBW, sentences, SUBW), F32),
            jax.ShapeDtypeStruct((cov_rows, width), F32),
        ),
        (received, proj),
        scalar=((dp_at * sub_count + sub_at) * cov_rows).reshape(1),
        name="combine",
    )


def solution(mesh):
    in_specs = (
        P("dp", "sub"),
        P("dp", None),
        P("dp"),
        P(None, "sub"),
        P(None, "sub"),
        P(None, "sub"),
        P("sub", None),
        P(None, "sub"),
        P("sub", None),
        P(),
        P(),
    )
    out_specs = (P("sub", "dp", None), P(("dp", "sub"), None))
    return jax.shard_map(
        on_device, mesh=mesh, in_specs=in_specs, out_specs=out_specs, check_vma=False
    )
```

```python
import functools
import math

import jax
import jax.numpy as jnp
from jax import lax
from jax.experimental import pallas as pl
from jax.experimental.pallas import tpu as pltpu
from jax.sharding import PartitionSpec as P

HDIM = 64
SUBW = 64
LANES = 128
SLOTS = 2
KINDS = 4
PACK = 8

epsilon = 1e-05
BF = jnp.bfloat16
F32 = jnp.float32
HIGH = lax.Precision.HIGHEST


def normalize(rows):
    center = jnp.mean(rows, axis=-1, keepdims=True)
    shifted = rows - center
    spread = jnp.mean(shifted * shifted, axis=-1, keepdims=True)
    return shifted * lax.rsqrt(spread + epsilon)


def dot(a, b, dims=((1,), (0,)), precision=None):
    return lax.dot_general(a, b, (dims, ((), ())), precision=precision, preferred_element_type=F32)


def split(array):
    high = array.astype(BF)
    return high, (array - high.astype(F32)).astype(BF)


def cost(flops, size):
    return pl.CostEstimate(flops=flops, bytes_accessed=size, transcendentals=0)


def attention_kernel(offsets, parts, chunk, with_base, me_ref, ends_ref, *refs):
    pieces, (w_ref, wo_ref), (out_ref, rows_ref, sems) = refs[:parts + 1], refs[parts + 1:parts + 3], refs[parts + 3:]
    me = me_ref[0]
    half = parts // 2
    part = pieces[0].shape[1]
    chunks = [lax.rem(me + (off + parts), parts) for off in offsets]

    def slot(i, away):
        at = lax.rem(me + (away + parts), parts)
        return rows_ref.at[i, :, pl.ds(pl.multiple_of(at * part, part), part)]

    def fetch(source, start, i, away, number):
        start = pl.multiple_of(start, chunk)
        return pltpu.make_async_copy(source.at[pl.ds(start, chunk), :], slot(i, away), sems.at[i, number])

    for i, c in enumerate(chunks):
        for k in range(half):
            fetch(pieces[k], c * chunk, i, k, k).start()
        for k in range(1, half):
            fetch(pieces[half + 1 + k], c * chunk, i, -k, half + k).start()

        @pl.when(c < half)
        def _():
            fetch(pieces[half], c * chunk, i, half, half).start()

        @pl.when(c >= half)
        def _():
            fetch(pieces[half + 1], (c - half) * chunk, i, half, half).start()

    for i, c in enumerate(chunks):
        for k in range(half):
            fetch(pieces[k], c * chunk, i, k, k).wait()
        for k in range(1, half):
            fetch(pieces[half + 1 + k], c * chunk, i, -k, half + k).wait()
        fetch(pieces[half], 0, i, half, half).wait()
    count = len(offsets)
    rows = rows_ref[...].reshape(count * chunk, -1).astype(F32)
    normed = normalize(rows).astype(BF)
    projected = dot(normed, w_ref[...]).astype(BF)
    local = wo_ref.shape[0]
    block_rows = chunk * parts // ends_ref.shape[0]
    blocks = chunk // block_rows
    per_block = ends_ref.shape[1]

    def keys(c, shape, axis):
        row = lax.broadcasted_iota(jnp.int32, shape, axis)
        block = row // block_rows
        key = block * per_block
        for b in range(blocks):
            for e in range(per_block - 1):
                end = ends_ref[c * blocks + b, e] + b * block_rows
                key = key + jnp.where((block == b) & (row >= end), 1, 0)
        return key

    lines = []
    for i, c in enumerate(chunks):
        mine = projected[i * chunk:(i + 1) * chunk]
        matches = keys(c, (chunk, 1), 0) == keys(c, (1, chunk), 1)
        heads = []
        for h in range(local // HDIM):
            query, key, value = (
                mine[:, t * local + h * HDIM:t * local + (h + 1) * HDIM] for t in range(3)
            )
            scores = dot(query, key, ((1,), (1,))) / math.sqrt(HDIM)
            raised = jnp.where(matches, jnp.exp(scores), 0.0)
            weights = (raised / jnp.sum(raised, axis=-1, keepdims=True)).astype(BF)
            heads.append(dot(weights, value).astype(BF))
        lines.append(jnp.concatenate(heads, axis=-1))
    context = jnp.concatenate(lines, axis=0)
    if with_base:
        out_ref[...] = rows + dot(context, wo_ref[...])
    else:
        out_ref[...] = context


def attention(pieces, w_qkv, w_out, ends, me, offsets, with_base=False):
    parts = len(pieces) - 1
    count, part = pieces[0].shape
    chunk = count // parts
    local, width = w_out.shape
    size = len(offsets)
    smem = pl.BlockSpec(memory_space=pltpu.SMEM)
    vmem = pl.BlockSpec(memory_space=pltpu.VMEM)
    hbm = pl.BlockSpec(memory_space=pltpu.HBM)
    pieces = [pltpu.with_memory_space_constraint(p, pltpu.HBM) for p in pieces]
    return pl.pallas_call(
        functools.partial(attention_kernel, offsets, parts, chunk, with_base),
        in_specs=[smem, smem] + [hbm] * len(pieces) + [vmem] * 2,
        out_specs=vmem,
        out_shape=jax.ShapeDtypeStruct((size * chunk, width if with_base else local), F32 if with_base else BF),
        scratch_shapes=[pltpu.VMEM((size, chunk, width), BF), pltpu.SemaphoreType.DMA((size, parts))],
        compiler_params=pltpu.CompilerParams(vmem_limit_bytes=16 << 20),
        cost_estimate=cost(size * 2 * chunk * width * 4 * local, 3 << 20),
        name="attention",
    )(me, ends, *pieces, w_qkv, w_out)


def first_join_kernel(context_ref, wo_ref, right_ref, left_ref):
    half = right_ref.shape[0]
    sums = dot(context_ref[...], wo_ref[...]).astype(BF)
    right_ref[...] = sums[:half]
    left_ref[...] = sums[half:]


def join_kernel(context_ref, wo_ref, right_ref, left_ref, right_out, left_out):
    chunk = right_out.shape[0]
    sums = dot(context_ref[...], wo_ref[...])
    ahead, back = sums[:chunk], sums[chunk:]
    half = right_ref.shape[0]
    right_out[:half] = (ahead[:half] + right_ref[...].astype(F32)).astype(BF)
    left_out[chunk - half:] = (back[chunk - half:] + left_ref[...].astype(F32)).astype(BF)
    if half < chunk:
        right_out[half:] = ahead[half:].astype(BF)
        left_out[:chunk - half] = back[:chunk - half].astype(BF)


def middle_kernel(base_ref, right_ref, left_ref, hidden_ref, normed_ref):
    hidden = base_ref[...] + (right_ref[...].astype(F32) + left_ref[...].astype(F32))
    hidden_ref[...] = hidden
    normed_ref[...] = normalize(hidden).astype(BF)


def feed_kernel(own_ref, pair_ref, hidden_ref, up_ref, down_ref, gathered_ref, out_ref, send_ref, ups, downs, sems):
    count = own_ref.shape[0]
    planes = gathered_ref.shape[1]
    rows = gathered_ref.shape[2] // 2
    copies = [(pltpu.make_async_copy(up_ref, ups.at[0], sems.at[0, 0]),
               pltpu.make_async_copy(down_ref, downs.at[0], sems.at[0, 1]))]
    spread = gathered_ref.shape[0]
    for p in range(planes):
        copies.append(tuple(
            pltpu.make_async_copy(
                gathered_ref.at[:, p, t * rows:(t + 1) * rows, :],
                into.at[p + 1].reshape(spread, rows, into.shape[-1]),
                sems.at[p + 1, t],
            )
            for t, into in enumerate((ups, downs))
        ))
    for up, down in copies:
        up.start()
        down.start()
    both = jnp.concatenate([own_ref[...], pair_ref[...]], axis=0)
    total = None
    for p, (up, down) in enumerate(copies):
        up.wait()
        inner = jnp.maximum(dot(both, ups[p]), 0.0).astype(BF)
        down.wait()
        part = dot(inner, downs[p])
        total = part if total is None else total + part
    out_ref[...] = hidden_ref[...] + total[:count]
    send_ref[...] = total[count:].astype(BF)


def feed(own, pair, hidden1, w_up, w_down, gathered):
    planes = gathered.shape[1]
    count, width = own.shape
    hidden = w_up.shape[1]
    vmem = pl.BlockSpec(memory_space=pltpu.VMEM)
    hbm = pl.BlockSpec(memory_space=pltpu.HBM)
    w_up, w_down, gathered = (
        pltpu.with_memory_space_constraint(w, pltpu.HBM) for w in (w_up, w_down, gathered)
    )
    return pl.pallas_call(
        feed_kernel,
        in_specs=[vmem, vmem, vmem, hbm, hbm, hbm],
        out_specs=[vmem, vmem],
        out_shape=[jax.ShapeDtypeStruct(own.shape, F32), jax.ShapeDtypeStruct(own.shape, BF)],
        scratch_shapes=[
            pltpu.VMEM((planes + 1,) + w_up.shape, BF),
            pltpu.VMEM((planes + 1,) + w_down.shape, BF),
            pltpu.SemaphoreType.DMA((planes + 1, 2)),
        ],
        compiler_params=pltpu.CompilerParams(vmem_limit_bytes=24 << 20),
        cost_estimate=cost(8 * count * width * hidden * (planes + 1), 4 * (planes + 1) * width * hidden),
        name="feed",
    )(own, pair, hidden1, w_up, w_down, gathered)


def pool_kernel(hidden_ref, pair_ref, gain_ref, member_ref, length_ref, out_ref):
    hidden = hidden_ref[...] + pair_ref[...].astype(F32)
    finished = normalize(hidden) * gain_ref[...]
    pooled = dot(member_ref[...], finished, precision=HIGH) / length_ref[...]
    out_ref[...] = jnp.broadcast_to(pooled[None], out_ref.shape)


def moments_kernel(sub_ref, pooled_ref, proj_ref, code_ref, out_ref):
    me = sub_ref[0]
    parts, few, width = pooled_ref.shape
    sentences = parts * few
    pooled = pooled_ref[...].reshape(sentences, width)
    total = out_ref.shape[0]
    groups = total // PACK
    per_group = width // groups
    own = per_group // parts
    mean = jnp.mean(pooled, axis=0, keepdims=True)
    centred = pooled - mean
    feature = lax.broadcasted_iota(jnp.int32, (width, total), 0)
    wanted = lax.broadcasted_iota(jnp.int32, (width, total), 1)
    chosen = (wanted // PACK) * per_group + me * own + wanted % PACK
    pick = jnp.where((feature == chosen) & (wanted % PACK < own), 1.0, 0.0).astype(BF)
    large, small = split(centred)
    picked_large, picked_small = dot(large, pick).astype(BF), dot(small, pick).astype(BF)
    first = ((0,), (0,))
    moments = dot(picked_large, large, first) + (dot(picked_large, small, first) + dot(picked_small, large, first))
    rotated = dot(large, proj_ref[...]).astype(BF)
    lanes = rotated.shape[1]
    row = lax.broadcasted_iota(jnp.int32, (total, sentences), 0)
    pieces = []
    flags = []
    ones = jnp.ones((sentences, lanes), BF)
    for k in range(KINDS):
        place = (row % PACK == own + 2) & ((row // PACK) * KINDS + k == code_ref[...])
        place = jnp.where(place, 1.0, 0.0).astype(BF)
        pieces.append(dot(place, rotated))
        flags.append(dot(place, ones))
    sides = jnp.concatenate(pieces + flags, axis=-1)
    high = mean.astype(BF).astype(F32)
    low = mean - high
    line = lax.broadcasted_iota(jnp.int32, (total, 1), 0) % PACK
    means = jnp.where(line == own, high, 0.0) + jnp.where(line == own + 1, low, 0.0)
    out_ref[...] = (moments + means + sides).astype(BF)


def combine_kernel(where_ref, recv_ref, proj_ref, pq_ref, cov_ref):
    first = where_ref[0]
    own, width = cov_ref.shape
    recv = recv_ref[...]
    total = recv.shape[0]
    groups = total // PACK
    sentences = pq_ref.shape[1]
    count = float(groups * sentences)
    source = lax.broadcasted_iota(jnp.int32, (groups, total), 0)
    line = lax.broadcasted_iota(jnp.int32, (groups, total), 1)
    pick_mean = (line == source * PACK + own) | (line == source * PACK + own + 1)
    means = dot(jnp.where(pick_mean, 1.0, 0.0).astype(BF), recv)
    sides = dot(jnp.where(line == source * PACK + own + 2, 1.0, 0.0).astype(BF), recv)
    line = lax.broadcasted_iota(jnp.int32, (PACK, total), 1) % PACK
    within = dot(jnp.where(line == lax.broadcasted_iota(jnp.int32, (PACK, total), 0), 1.0, 0.0).astype(BF), recv)
    away = means - jnp.mean(means, axis=0, keepdims=True)
    feature = lax.broadcasted_iota(jnp.int32, (width, LANES), 0)
    lane = lax.broadcasted_iota(jnp.int32, (width, LANES), 1)
    pick = jnp.where((feature == first + lane) & (lane < own), 1.0, 0.0).astype(BF)
    large, small = split(away)
    picked_large, picked_small = dot(large, pick).astype(BF), dot(small, pick).astype(BF)
    rows = ((0,), (0,))
    between = dot(picked_large, large, rows) + (dot(picked_large, small, rows) + dot(picked_small, large, rows))
    cov_ref[...] = (within[:own] + float(sentences) * between[:own]) / count
    shift = dot(large, proj_ref[...]) + dot(small, proj_ref[...])
    shift_large, shift_small = split(shift)
    lanes = shift.shape[1]
    one = lax.broadcasted_iota(jnp.int32, (groups, groups), 0)
    other = lax.broadcasted_iota(jnp.int32, (groups, groups), 1)
    ahead = jnp.where(one < other, 1.0, 0.0).astype(BF)
    same = jnp.where(one == other, 1.0, 0.0).astype(BF)
    filled = [sides[:, (KINDS + 2 * c) * lanes:(KINDS + 2 * c + 1) * lanes] for c in range(SLOTS)]
    flat = [dot(f.astype(BF), same, ((0,), (0,)))[:1] for f in filled]
    before = dot((filled[0] + filled[1]).astype(BF), ahead, ((0,), (0,)))[:1]
    place = lax.broadcasted_iota(jnp.int32, (sentences, groups), 0)
    result = jnp.zeros((sentences, lanes), F32)
    for c in range(SLOTS):
        for k in range(2):
            rows = sides[:, (2 * c + k) * lanes:(2 * c + k + 1) * lanes].astype(BF)
            position = (2.0 * before + float(k)).astype(jnp.int32)
            chosen = jnp.where((place == position) & (flat[c] > 0.5), 1.0, 0.0).astype(BF)
            result = result + (dot(chosen, rows) + (dot(chosen, shift_large) + dot(chosen, shift_small)))
        before = before + flat[c]
    for q in range(pq_ref.shape[0]):
        pq_ref[q] = result[:, q * SUBW:(q + 1) * SUBW]


def small_call(kernel, outs, args, scalar=None, name=None):
    specs = [pl.BlockSpec(memory_space=pltpu.VMEM) for _ in args]
    if scalar is not None:
        specs = [pl.BlockSpec(memory_space=pltpu.SMEM)] + specs
        args = (scalar,) + tuple(args)
    single = not isinstance(outs, (tuple, list))
    return pl.pallas_call(
        kernel,
        in_specs=specs,
        out_specs=pl.BlockSpec(memory_space=pltpu.VMEM) if single else [pl.BlockSpec(memory_space=pltpu.VMEM) for _ in outs],
        out_shape=outs,
        compiler_params=pltpu.CompilerParams(vmem_limit_bytes=16 << 20),
        cost_estimate=cost(1 << 20, 1 << 20),
        name=name,
    )(*args)


def on_device(
    tokens, lengths, dest, w_query, w_key, w_value, w_out, w_up, w_down, final_gain, projection
):
    dp_count = lax.axis_size("dp")
    sub_count = lax.axis_size("sub")
    dp_at = lax.axis_index("dp")
    sub_at = lax.axis_index("sub")
    block_count, per_block = lengths.shape
    local_rows, local_width = tokens.shape
    block_rows = local_rows // block_count
    width = local_width * sub_count
    own_blocks = block_count // sub_count
    own_rows = own_blocks * block_rows
    half = sub_count // 2

    def move(array, by):
        return lax.ppermute(array, "sub", [(i, (i + by) % sub_count) for i in range(sub_count)])

    def swap(array):
        return lax.ppermute(array, "sub", [(i, i ^ 1) for i in range(sub_count)])

    rows = w_up.shape[0] // dp_count
    piece = jnp.concatenate(
        [lax.dynamic_slice_in_dim(w, dp_at * rows, rows, 0) for w in (w_up, w_down)], axis=0
    )
    piece, tokens = lax.optimization_barrier((piece, tokens))
    others = [move(piece, by) for by in range(2, sub_count, 2)]
    planes = half - 1

    ends = jnp.cumsum(lengths, axis=-1)
    position = jnp.arange(block_rows, dtype=jnp.int32)
    segment = jnp.sum((ends[:, None, :] <= position[None, :, None]).astype(jnp.int32), axis=-1)
    ordinal = jnp.arange(block_count, dtype=jnp.int32)
    keys = (ordinal[:, None] * per_block + segment).reshape(local_rows)
    own_lens = lax.dynamic_slice_in_dim(lengths, sub_at * own_blocks, own_blocks, 0)
    own_keys = lax.dynamic_slice_in_dim(keys, sub_at * own_rows, own_rows, 0)
    own_sentences = own_blocks * per_block
    member = (
        own_keys[None, :] == sub_at * own_sentences + jnp.arange(own_sentences, dtype=jnp.int32)[:, None]
    ).astype(F32)
    matches = dest[:, None] == dest[None, :]
    earlier = ordinal[:, None] > ordinal[None, :]
    earlier_count = jnp.sum((matches & earlier).astype(jnp.int32), axis=1)
    code = (dest * SLOTS + earlier_count)[:, None] * per_block + jnp.arange(per_block, dtype=jnp.int32)[None, :]
    code = code.reshape(1, block_count * per_block)
    w_qkv = jnp.concatenate((w_query, w_key, w_value), axis=1)
    columns = width // sub_count
    proj = lax.dynamic_slice_in_dim(projection, sub_at * columns, columns, 1)

    behind, ahead = [], []
    right = left = tokens
    for step in range(half - 1):
        right, left = move(right, 1), move(left, -1)
        if step == 0:
            others = lax.optimization_barrier((others, right, left))[0]
        behind.append(right)
        ahead.append(left)
    middle = local_rows // 2
    far = [move(right[:middle], 1), move(left[middle:], -1)]
    pieces = [tokens] + ahead + far + behind

    gathered = lax.all_gather(jnp.concatenate(others, axis=0), "dp", axis=0, tiled=True)
    gathered = gathered.reshape(dp_count, planes, 2 * rows, width)

    attend = functools.partial(attention, pieces, w_qkv, w_out, ends, sub_at.reshape(1))
    own_shape = (own_rows, width)
    half_shape = (own_rows // 2, width)
    right, left = small_call(
        first_join_kernel,
        [jax.ShapeDtypeStruct(half_shape, BF)] * 2,
        (attend([half]), w_out),
        name="join",
    )
    right, left = move(right, 1), move(left, -1)
    for away in range(half - 1, 0, -1):
        right, left = small_call(
            join_kernel,
            [jax.ShapeDtypeStruct(own_shape, BF)] * 2,
            (attend([away, -away]), w_out, right, left),
            name="join",
        )
        right, left = move(right, 1), move(left, -1)
    base = attend([0], with_base=True)
    hidden1, normed2 = small_call(
        middle_kernel,
        (jax.ShapeDtypeStruct(own_shape, F32), jax.ShapeDtypeStruct(own_shape, BF)),
        (base, right, left),
        name="middle",
    )
    hidden2, sent = feed(normed2, swap(normed2), hidden1, w_up, w_down, gathered)
    pooled = small_call(
        pool_kernel,
        jax.ShapeDtypeStruct((sub_count, own_sentences, width), F32),
        (hidden2, swap(sent), final_gain[None, :], member, own_lens.reshape(own_sentences, 1).astype(F32)),
        name="pool",
    )
    pooled = lax.all_to_all(pooled, "sub", split_axis=0, concat_axis=0, tiled=True)
    sentences = sub_count * own_sentences
    cov_rows = width // (dp_count * sub_count)
    sent = small_call(
        moments_kernel,
        jax.ShapeDtypeStruct((dp_count * PACK, width), BF),
        (pooled, proj, code),
        scalar=sub_at.reshape(1),
        name="moments",
    )
    received = lax.all_to_all(
        sent.reshape(dp_count, PACK, width), "dp", split_axis=0, concat_axis=0, tiled=True
    ).reshape(dp_count * PACK, width)
    return small_call(
        combine_kernel,
        (
            jax.ShapeDtypeStruct((columns // SUBW, sentences, SUBW), F32),
            jax.ShapeDtypeStruct((cov_rows, width), F32),
        ),
        (received, proj),
        scalar=((dp_at * sub_count + sub_at) * cov_rows).reshape(1),
        name="combine",
    )


def solution(mesh):
    in_specs = (
        P("dp", "sub"),
        P("dp", None),
        P("dp"),
        P(None, "sub"),
        P(None, "sub"),
        P(None, "sub"),
        P("sub", None),
        P(None, "sub"),
        P("sub", None),
        P(),
        P(),
    )
    out_specs = (P("sub", "dp", None), P(("dp", "sub"), None))
    return jax.shard_map(
        on_device, mesh=mesh, in_specs=in_specs, out_specs=out_specs, check_vma=False
    )
```

```python
import functools
import math

import jax
import jax.numpy as jnp
from jax import lax
from jax.experimental import pallas as pl
from jax.experimental.pallas import tpu as pltpu
from jax.sharding import PartitionSpec as P

HDIM = 64
SUBW = 64
LANES = 128
SLOTS = 2
CORES = 2
KINDS = 4
PACK = 8

epsilon = 1e-05
BF = jnp.bfloat16
F32 = jnp.float32
HIGH = lax.Precision.HIGHEST


def normalize(rows):
    center = jnp.mean(rows, axis=-1, keepdims=True)
    shifted = rows - center
    spread = jnp.mean(shifted * shifted, axis=-1, keepdims=True)
    return shifted * lax.rsqrt(spread + epsilon)


def dot(a, b, dims=((1,), (0,)), precision=None):
    return lax.dot_general(a, b, (dims, ((), ())), precision=precision, preferred_element_type=F32)


def split(array):
    high = array.astype(BF)
    return high, (array - high.astype(F32)).astype(BF)


def cost(flops, size):
    return pl.CostEstimate(flops=flops, bytes_accessed=size, transcendentals=0)


def attention_kernel(offsets, parts, chunk, with_base, me_ref, ends_ref, *refs):
    pieces, (w_ref, wo_ref), (out_ref, rows_ref, sems) = refs[:parts + 1], refs[parts + 1:parts + 3], refs[parts + 3:]
    me = me_ref[0]
    half = parts // 2
    part = pieces[0].shape[1]
    chunks = [lax.rem(me + (off + parts), parts) for off in offsets]

    def slot(i, away):
        at = lax.rem(me + (away + parts), parts)
        return rows_ref.at[i, :, pl.ds(pl.multiple_of(at * part, part), part)]

    def fetch(source, start, i, away, number):
        start = pl.multiple_of(start, chunk)
        return pltpu.make_async_copy(source.at[pl.ds(start, chunk), :], slot(i, away), sems.at[i, number])

    for i, c in enumerate(chunks):
        for k in range(half):
            fetch(pieces[k], c * chunk, i, k, k).start()
        for k in range(1, half):
            fetch(pieces[half + 1 + k], c * chunk, i, -k, half + k).start()

        @pl.when(c < half)
        def _():
            fetch(pieces[half], c * chunk, i, half, half).start()

        @pl.when(c >= half)
        def _():
            fetch(pieces[half + 1], (c - half) * chunk, i, half, half).start()

    for i, c in enumerate(chunks):
        for k in range(half):
            fetch(pieces[k], c * chunk, i, k, k).wait()
        for k in range(1, half):
            fetch(pieces[half + 1 + k], c * chunk, i, -k, half + k).wait()
        fetch(pieces[half], 0, i, half, half).wait()
    count = len(offsets)
    rows = rows_ref[...].reshape(count * chunk, -1).astype(F32)
    normed = normalize(rows).astype(BF)
    projected = dot(normed, w_ref[...]).astype(BF)
    local = wo_ref.shape[0]
    block_rows = chunk * parts // ends_ref.shape[0]
    blocks = chunk // block_rows
    per_block = ends_ref.shape[1]

    def keys(c, shape, axis):
        row = lax.broadcasted_iota(jnp.int32, shape, axis)
        block = row // block_rows
        key = block * per_block
        for b in range(blocks):
            for e in range(per_block - 1):
                end = ends_ref[c * blocks + b, e] + b * block_rows
                key = key + jnp.where((block == b) & (row >= end), 1, 0)
        return key

    lines = []
    for i, c in enumerate(chunks):
        mine = projected[i * chunk:(i + 1) * chunk]
        matches = keys(c, (chunk, 1), 0) == keys(c, (1, chunk), 1)
        heads = []
        for h in range(local // HDIM):
            query, key, value = (
                mine[:, t * local + h * HDIM:t * local + (h + 1) * HDIM] for t in range(3)
            )
            scores = dot(query, key, ((1,), (1,))) / math.sqrt(HDIM)
            raised = jnp.where(matches, jnp.exp(scores), 0.0)
            weights = (raised / jnp.sum(raised, axis=-1, keepdims=True)).astype(BF)
            heads.append(dot(weights, value).astype(BF))
        lines.append(jnp.concatenate(heads, axis=-1))
    context = jnp.concatenate(lines, axis=0)
    if with_base:
        out_ref[...] = rows + dot(context, wo_ref[...])
    else:
        out_ref[...] = context


def attention(pieces, w_qkv, w_out, ends, me, offsets, with_base=False):
    parts = len(pieces) - 1
    count, part = pieces[0].shape
    chunk = count // parts
    local, width = w_out.shape
    size = len(offsets)
    smem = pl.BlockSpec(memory_space=pltpu.SMEM)
    vmem = pl.BlockSpec(memory_space=pltpu.VMEM)
    hbm = pl.BlockSpec(memory_space=pltpu.HBM)
    pieces = [pltpu.with_memory_space_constraint(p, pltpu.HBM) for p in pieces]
    return pl.pallas_call(
        functools.partial(attention_kernel, offsets, parts, chunk, with_base),
        in_specs=[smem, smem] + [hbm] * len(pieces) + [vmem] * 2,
        out_specs=vmem,
        out_shape=jax.ShapeDtypeStruct((size * chunk, width if with_base else local), F32 if with_base else BF),
        scratch_shapes=[pltpu.VMEM((size, chunk, width), BF), pltpu.SemaphoreType.DMA((size, parts))],
        compiler_params=pltpu.CompilerParams(vmem_limit_bytes=16 << 20),
        cost_estimate=cost(40 * size * 2 * chunk * width * 4 * local, 3 << 20),
        name="attention",
    )(me, ends, *pieces, w_qkv, w_out)


def first_join_kernel(context_ref, wo_ref, right_ref, left_ref):
    half = right_ref.shape[0]
    sums = dot(context_ref[...], wo_ref[...]).astype(BF)
    right_ref[...] = sums[:half]
    left_ref[...] = sums[half:]


def join_kernel(at, start, context_ref, wo_ref, recv_ref, out_ref):
    chunk, half = out_ref.shape[0], recv_ref.shape[0]
    sums = dot(context_ref[at * chunk:(at + 1) * chunk], wo_ref[...])
    rows = slice(start, start + half)
    out_ref[rows] = (sums[rows] + recv_ref[...].astype(F32)).astype(BF)
    if half < chunk:
        rest = slice(half - start, chunk - start)
        out_ref[rest] = sums[rest].astype(BF)


def middle_kernel(base_ref, right_ref, left_ref, hidden_ref, normed_ref):
    hidden = base_ref[...] + (right_ref[...].astype(F32) + left_ref[...].astype(F32))
    hidden_ref[...] = hidden
    normed_ref[...] = normalize(hidden).astype(BF)


def feed_kernel(own_ref, pair_ref, hidden_ref, up_ref, down_ref, gathered_ref, out_ref, send_ref, ups, downs, sems):
    count = own_ref.shape[0]
    planes = gathered_ref.shape[1]
    rows = gathered_ref.shape[2] // 2
    copies = [(pltpu.make_async_copy(up_ref, ups.at[0], sems.at[0, 0]),
               pltpu.make_async_copy(down_ref, downs.at[0], sems.at[0, 1]))]
    spread = gathered_ref.shape[0]
    for p in range(planes):
        copies.append(tuple(
            pltpu.make_async_copy(
                gathered_ref.at[:, p, t * rows:(t + 1) * rows, :],
                into.at[p + 1].reshape(spread, rows, into.shape[-1]),
                sems.at[p + 1, t],
            )
            for t, into in enumerate((ups, downs))
        ))
    for up, down in copies:
        up.start()
        down.start()
    both = jnp.concatenate([own_ref[...], pair_ref[...]], axis=0)
    total = None
    for p, (up, down) in enumerate(copies):
        up.wait()
        inner = jnp.maximum(dot(both, ups[p]), 0.0).astype(BF)
        down.wait()
        part = dot(inner, downs[p])
        total = part if total is None else total + part
    out_ref[...] = hidden_ref[...] + total[:count]
    send_ref[...] = total[count:].astype(BF)


def feed(own, pair, hidden1, w_up, w_down, gathered):
    planes = gathered.shape[1]
    count, width = own.shape
    hidden = w_up.shape[1]
    vmem = pl.BlockSpec(memory_space=pltpu.VMEM)
    hbm = pl.BlockSpec(memory_space=pltpu.HBM)
    w_up, w_down, gathered = (
        pltpu.with_memory_space_constraint(w, pltpu.HBM) for w in (w_up, w_down, gathered)
    )
    return pl.pallas_call(
        feed_kernel,
        in_specs=[vmem, vmem, vmem, hbm, hbm, hbm],
        out_specs=[vmem, vmem],
        out_shape=[jax.ShapeDtypeStruct(own.shape, F32), jax.ShapeDtypeStruct(own.shape, BF)],
        scratch_shapes=[
            pltpu.VMEM((planes + 1,) + w_up.shape, BF),
            pltpu.VMEM((planes + 1,) + w_down.shape, BF),
            pltpu.SemaphoreType.DMA((planes + 1, 2)),
        ],
        compiler_params=pltpu.CompilerParams(vmem_limit_bytes=24 << 20),
        cost_estimate=cost(8 * count * width * hidden * (planes + 1), 4 * (planes + 1) * width * hidden),
        name="feed",
    )(own, pair, hidden1, w_up, w_down, gathered)


def pool_kernel(hidden_ref, pair_ref, gain_ref, member_ref, length_ref, out_ref):
    hidden = hidden_ref[...] + pair_ref[...].astype(F32)
    finished = normalize(hidden) * gain_ref[...]
    pooled = dot(member_ref[...], finished, precision=HIGH) / length_ref[...]
    out_ref[...] = jnp.broadcast_to(pooled[None], out_ref.shape)


def moments_kernel(own, where_ref, pooled_ref, proj_ref, code_ref, out_ref):
    first, core = where_ref[0], where_ref[1]
    parts, few, width = pooled_ref.shape
    sentences = parts * few
    pooled = pooled_ref[...].reshape(sentences, width)
    total = out_ref.shape[0]
    per_chip = width // (total // PACK)
    mean = jnp.mean(pooled, axis=0, keepdims=True)
    large, small = split(pooled - mean)
    feature = lax.broadcasted_iota(jnp.int32, (width, total), 0)
    wanted = lax.broadcasted_iota(jnp.int32, (width, total), 1)
    chosen = (wanted // PACK) * per_chip + first + wanted % PACK
    pick = jnp.where((feature == chosen) & (wanted % PACK < own), 1.0, 0.0).astype(BF)
    picked_large, picked_small = dot(large, pick).astype(BF), dot(small, pick).astype(BF)
    rows = ((0,), (0,))
    moments = dot(picked_large, large, rows) + (dot(picked_large, small, rows) + dot(picked_small, large, rows))
    rotated = dot(large, proj_ref[...]).astype(BF)
    lanes = rotated.shape[1]
    row = lax.broadcasted_iota(jnp.int32, (total, sentences), 0)
    column = lax.broadcasted_iota(jnp.int32, (total, sentences), 1)
    target = ((row // PACK) * CORES + core) * KINDS
    half = sentences // CORES
    ones = jnp.ones((sentences, lanes), BF)
    sides = []
    for a in range(CORES):
        mine = (column // half == a) & (row % PACK == own + 2)
        there = (column // half == a) & (row % PACK == own + 3)
        for k in range(KINDS):
            hit = target + k == code_ref[...]
            sides.append(
                dot(jnp.where(mine & hit, 1.0, 0.0).astype(BF), rotated)
                + dot(jnp.where(there & hit, 1.0, 0.0).astype(BF), ones)
            )
    sides = jnp.concatenate(sides, axis=-1)
    high = mean.astype(BF).astype(F32)
    low = mean - high
    line = lax.broadcasted_iota(jnp.int32, (total, 1), 0) % PACK
    means = jnp.where(line == own, high, 0.0) + jnp.where(line == own + 1, low, 0.0)
    out_ref[...] = (moments + means + sides).astype(BF)


def combine_kernel(where_ref, recv_ref, proj_ref, pq_ref, cov_ref):
    first = where_ref[0]
    own, width = cov_ref.shape
    recv = recv_ref[...]
    total = recv.shape[0]
    chips = total // PACK
    sentences = pq_ref.shape[1]
    each = float(CORES * sentences)
    source = lax.broadcasted_iota(jnp.int32, (chips, total), 0)
    line = lax.broadcasted_iota(jnp.int32, (chips, total), 1) - source * PACK
    means = dot(jnp.where((line == own) | (line == own + 1), 1.0, 0.0).astype(BF), recv)
    sides = dot(jnp.where(line == own + 2, 1.0, 0.0).astype(BF), recv).astype(BF)
    there = dot(jnp.where(line == own + 3, 1.0, 0.0).astype(BF), recv).astype(BF)
    line = lax.broadcasted_iota(jnp.int32, (PACK, total), 1) % PACK
    within = dot(jnp.where(line == lax.broadcasted_iota(jnp.int32, (PACK, total), 0), 1.0, 0.0).astype(BF), recv)
    away = means - jnp.mean(means, axis=0, keepdims=True)
    feature = lax.broadcasted_iota(jnp.int32, (width, LANES), 0)
    lane = lax.broadcasted_iota(jnp.int32, (width, LANES), 1)
    pick = jnp.where((feature == first + lane) & (lane < own), 1.0, 0.0).astype(BF)
    large, small = split(away)
    picked_large, picked_small = dot(large, pick).astype(BF), dot(small, pick).astype(BF)
    rows = ((0,), (0,))
    between = dot(picked_large, large, rows) + (dot(picked_large, small, rows) + dot(picked_small, large, rows))
    cov_ref[...] = (within[:own] + each * between[:own]) / (each * float(chips))
    shift = dot(large, proj_ref[...]) + dot(small, proj_ref[...])
    shift_large, shift_small = split(shift)
    lanes = shift.shape[1]
    one = lax.broadcasted_iota(jnp.int32, (chips, chips), 0)
    other = lax.broadcasted_iota(jnp.int32, (chips, chips), 1)
    ahead = jnp.where(one < other, 1.0, 0.0).astype(BF)
    same = jnp.where(one == other, 1.0, 0.0).astype(BF)
    kinds = [a * KINDS + 2 * c for a in range(CORES) for c in range(SLOTS)]
    filled = [there[:, k * lanes:(k + 1) * lanes] for k in kinds]
    flat = [dot(f, same, ((0,), (0,)))[:1] for f in filled]
    before = sum(dot(f, ahead, ((0,), (0,)))[:1] for f in filled)
    place = lax.broadcasted_iota(jnp.int32, (sentences, chips), 0)
    result = jnp.zeros((sentences, lanes), F32)
    for kind, here in zip(kinds, flat):
        for k in range(2):
            position = (2.0 * before + float(k)).astype(jnp.int32)
            chosen = jnp.where((place == position) & (here > 0.5), 1.0, 0.0).astype(BF)
            block = sides[:, (kind + k) * lanes:(kind + k + 1) * lanes]
            result = result + (dot(chosen, block) + (dot(chosen, shift_large) + dot(chosen, shift_small)))
        before = before + here
    for q in range(pq_ref.shape[0]):
        pq_ref[q] = result[:, q * SUBW:(q + 1) * SUBW]


def small_call(kernel, outs, args, scalar=None, name=None):
    specs = [pl.BlockSpec(memory_space=pltpu.VMEM) for _ in args]
    if scalar is not None:
        specs = [pl.BlockSpec(memory_space=pltpu.SMEM)] + specs
        args = (scalar,) + tuple(args)
    single = not isinstance(outs, (tuple, list))
    return pl.pallas_call(
        kernel,
        in_specs=specs,
        out_specs=pl.BlockSpec(memory_space=pltpu.VMEM) if single else [pl.BlockSpec(memory_space=pltpu.VMEM) for _ in outs],
        out_shape=outs,
        compiler_params=pltpu.CompilerParams(vmem_limit_bytes=16 << 20),
        cost_estimate=cost(1 << 20, 1 << 20),
        name=name,
    )(*args)


def on_device(
    tokens, lengths, dest, w_query, w_key, w_value, w_out, w_up, w_down, final_gain, projection
):
    dp_count = lax.axis_size("dp")
    sub_count = lax.axis_size("sub")
    dp_at = lax.axis_index("dp")
    sub_at = lax.axis_index("sub")
    block_count, per_block = lengths.shape
    local_rows, local_width = tokens.shape
    block_rows = local_rows // block_count
    width = local_width * sub_count
    own_blocks = block_count // sub_count
    own_rows = own_blocks * block_rows
    half = sub_count // 2

    def move(array, by):
        return lax.ppermute(array, "sub", [(i, (i + by) % sub_count) for i in range(sub_count)])

    def swap(array):
        return lax.ppermute(array, "sub", [(i, i ^ 1) for i in range(sub_count)])

    rows = w_up.shape[0] // dp_count
    piece = jnp.concatenate(
        [lax.dynamic_slice_in_dim(w, dp_at * rows, rows, 0) for w in (w_up, w_down)], axis=0
    )
    piece, tokens = lax.optimization_barrier((piece, tokens))
    across = lax.ppermute(
        piece, "sub", [(i, (i + (half - 1 if i % 2 else 1 - half)) % sub_count) for i in range(sub_count)]
    )
    others = [move(piece, 2), move(piece, -2), across]
    planes = len(others)

    ends = jnp.cumsum(lengths, axis=-1)
    position = jnp.arange(block_rows, dtype=jnp.int32)
    segment = jnp.sum((ends[:, None, :] <= position[None, :, None]).astype(jnp.int32), axis=-1)
    ordinal = jnp.arange(block_count, dtype=jnp.int32)
    keys = (ordinal[:, None] * per_block + segment).reshape(local_rows)
    own_lens = lax.dynamic_slice_in_dim(lengths, sub_at * own_blocks, own_blocks, 0)
    own_keys = lax.dynamic_slice_in_dim(keys, sub_at * own_rows, own_rows, 0)
    own_sentences = own_blocks * per_block
    member = (
        own_keys[None, :] == sub_at * own_sentences + jnp.arange(own_sentences, dtype=jnp.int32)[:, None]
    ).astype(F32)
    matches = dest[:, None] == dest[None, :]
    earlier = ordinal[:, None] > ordinal[None, :]
    earlier_count = jnp.sum((matches & earlier).astype(jnp.int32), axis=1)
    code = (dest * SLOTS + earlier_count)[:, None] * per_block + jnp.arange(per_block, dtype=jnp.int32)[None, :]
    code = code.reshape(1, block_count * per_block)
    chips = dp_count // CORES
    siblings = [[q * CORES + c for c in range(CORES)] for q in range(chips)]
    other = lax.ppermute(code, "dp", [(i, i ^ 1) for i in range(dp_count)])
    core = dp_at % CORES
    code = jnp.where(core == 0, jnp.concatenate((code, other), axis=1), jnp.concatenate((other, code), axis=1))
    w_qkv = jnp.concatenate((w_query, w_key, w_value), axis=1)
    columns = width // sub_count
    proj = lax.dynamic_slice_in_dim(projection, sub_at * columns, columns, 1)

    behind, ahead = [], []
    right = left = tokens
    for step in range(half - 1):
        right, left = move(right, 1), move(left, -1)
        if step == 0:
            others = lax.optimization_barrier((others, right, left))[0]
        behind.append(right)
        ahead.append(left)
    halfway = local_rows // 2
    far = [move(right[:halfway], 1), move(left[halfway:], -1)]
    pieces = [tokens] + ahead + far + behind

    gathered = lax.all_gather(jnp.concatenate(others, axis=0), "dp", axis=0, tiled=True)
    gathered = gathered.reshape(dp_count, planes, 2 * rows, width)

    attend = functools.partial(attention, pieces, w_qkv, w_out, ends, sub_at.reshape(1))
    own_shape = (own_rows, width)
    half_shape = (own_rows // 2, width)
    right, left = small_call(
        first_join_kernel,
        [jax.ShapeDtypeStruct(half_shape, BF)] * 2,
        (attend([half]), w_out),
        name="join",
    )
    right, left = move(right, 1), move(left, -1)
    for away in range(half - 1, 0, -1):
        context = attend([away, -away])
        join = lambda at, start, recv: small_call(
            functools.partial(join_kernel, at, start),
            jax.ShapeDtypeStruct(own_shape, BF),
            (context, w_out, recv),
            name="join",
        )
        right, left = move(join(0, 0, right), 1), move(join(1, own_rows - left.shape[0], left), -1)
    base = attend([0], with_base=True)
    hidden1, normed2 = small_call(
        middle_kernel,
        (jax.ShapeDtypeStruct(own_shape, F32), jax.ShapeDtypeStruct(own_shape, BF)),
        (base, right, left),
        name="middle",
    )
    hidden2, sent = feed(normed2, swap(normed2), hidden1, w_up, w_down, gathered)
    pooled = small_call(
        pool_kernel,
        jax.ShapeDtypeStruct((sub_count, own_sentences, width), F32),
        (hidden2, swap(sent), final_gain[None, :], member, own_lens.reshape(own_sentences, 1).astype(F32)),
        name="pool",
    )
    pooled = lax.all_to_all(pooled, "sub", split_axis=0, concat_axis=0, tiled=True)
    pooled = lax.all_gather(pooled, "dp", axis=0, tiled=True, axis_index_groups=siblings)
    sentences = sub_count * own_sentences
    cov_rows = width // (dp_count * sub_count)
    sent = small_call(
        functools.partial(moments_kernel, cov_rows),
        jax.ShapeDtypeStruct((chips * PACK, width), BF),
        (pooled, proj, code),
        scalar=jnp.stack([(core * sub_count + sub_at) * cov_rows, core]).astype(jnp.int32),
        name="moments",
    )
    received = lax.all_to_all(
        sent.reshape(chips, PACK, width), "dp", split_axis=0, concat_axis=0, tiled=True,
        axis_index_groups=[[q * CORES + c for q in range(chips)] for c in range(CORES)],
    ).reshape(chips * PACK, width)
    return small_call(
        combine_kernel,
        (
            jax.ShapeDtypeStruct((columns // SUBW, sentences, SUBW), F32),
            jax.ShapeDtypeStruct((cov_rows, width), F32),
        ),
        (received, proj),
        scalar=((dp_at * sub_count + sub_at) * cov_rows).reshape(1),
        name="combine",
    )


def solution(mesh):
    in_specs = (
        P("dp", "sub"),
        P("dp", None),
        P("dp"),
        P(None, "sub"),
        P(None, "sub"),
        P(None, "sub"),
        P("sub", None),
        P(None, "sub"),
        P("sub", None),
        P(),
        P(),
    )
    out_specs = (P("sub", "dp", None), P(("dp", "sub"), None))
    return jax.shard_map(
        on_device, mesh=mesh, in_specs=in_specs, out_specs=out_specs, check_vma=False
    )
```

```python
import functools
import math

import jax
import jax.numpy as jnp
from jax import lax
from jax.experimental import pallas as pl
from jax.experimental.pallas import tpu as pltpu
from jax.sharding import PartitionSpec as P

HDIM = 64
SUBW = 64
LANES = 128
SLOTS = 2
CORES = 2
KINDS = 4
PACK = 8

epsilon = 1e-05
BF = jnp.bfloat16
F32 = jnp.float32
HIGH = lax.Precision.HIGHEST


def normalize(rows):
    center = jnp.mean(rows, axis=-1, keepdims=True)
    shifted = rows - center
    spread = jnp.mean(shifted * shifted, axis=-1, keepdims=True)
    return shifted * lax.rsqrt(spread + epsilon)


def dot(a, b, dims=((1,), (0,)), precision=None):
    return lax.dot_general(a, b, (dims, ((), ())), precision=precision, preferred_element_type=F32)


def split(array):
    high = array.astype(BF)
    return high, (array - high.astype(F32)).astype(BF)


def cost(flops, size):
    return pl.CostEstimate(flops=flops, bytes_accessed=size, transcendentals=0)


def attention_kernel(offsets, parts, chunk, with_base, me_ref, ends_ref, *refs):
    pieces, (wq_ref, wk_ref, wv_ref, wo_ref), rest = refs[:parts + 1], refs[parts + 1:parts + 5], refs[parts + 5:]
    out_ref, rows_ref, sems = rest
    me = me_ref[0]
    half = parts // 2
    part = pieces[0].shape[1]
    chunks = [lax.rem(me + (off + parts), parts) for off in offsets]

    def slot(i, away):
        at = lax.rem(me + (away + parts), parts)
        return rows_ref.at[i, :, pl.ds(pl.multiple_of(at * part, part), part)]

    def fetch(source, start, i, away, number):
        start = pl.multiple_of(start, chunk)
        return pltpu.make_async_copy(source.at[pl.ds(start, chunk), :], slot(i, away), sems.at[i, number])

    for i, c in enumerate(chunks):
        for k in range(half):
            fetch(pieces[k], c * chunk, i, k, k).start()
        for k in range(1, half):
            fetch(pieces[half + 1 + k], c * chunk, i, -k, half + k).start()

        @pl.when(c < half)
        def _():
            fetch(pieces[half], c * chunk, i, half, half).start()

        @pl.when(c >= half)
        def _():
            fetch(pieces[half + 1], (c - half) * chunk, i, half, half).start()

    for i, c in enumerate(chunks):
        for k in range(half):
            fetch(pieces[k], c * chunk, i, k, k).wait()
        for k in range(1, half):
            fetch(pieces[half + 1 + k], c * chunk, i, -k, half + k).wait()
        fetch(pieces[half], 0, i, half, half).wait()
    count = len(offsets)
    rows = rows_ref[...].reshape(count * chunk, -1).astype(F32)
    normed = normalize(rows).astype(BF)
    w_qkv = jnp.concatenate([wq_ref[...], wk_ref[...], wv_ref[...]], axis=1)
    projected = dot(normed, w_qkv).astype(BF)
    local = wo_ref.shape[0]
    block_rows = chunk * parts // ends_ref.shape[1]
    blocks = chunk // block_rows
    per_block = ends_ref.shape[0]

    def keys(c, shape, axis):
        row = lax.broadcasted_iota(jnp.int32, shape, axis)
        block = row // block_rows
        key = block * per_block
        for b in range(blocks):
            end = b * block_rows
            for e in range(per_block - 1):
                end = end + ends_ref[e, c * blocks + b]
                key = key + jnp.where((block == b) & (row >= end), 1, 0)
        return key

    lines = []
    for i, c in enumerate(chunks):
        mine = projected[i * chunk:(i + 1) * chunk]
        matches = keys(c, (chunk, 1), 0) == keys(c, (1, chunk), 1)
        heads = []
        for h in range(local // HDIM):
            query, key, value = (
                mine[:, t * local + h * HDIM:t * local + (h + 1) * HDIM] for t in range(3)
            )
            scores = dot(query, key, ((1,), (1,))) / math.sqrt(HDIM)
            raised = jnp.where(matches, jnp.exp(scores), 0.0)
            weights = (raised / jnp.sum(raised, axis=-1, keepdims=True)).astype(BF)
            heads.append(dot(weights, value).astype(BF))
        lines.append(jnp.concatenate(heads, axis=-1))
    context = jnp.concatenate(lines, axis=0)
    if with_base:
        out_ref[...] = rows + dot(context, wo_ref[...])
    else:
        out_ref[...] = context


def attention(pieces, weights, w_out, ends, me, offsets, with_base=False):
    parts = len(pieces) - 1
    count, part = pieces[0].shape
    chunk = count // parts
    local, width = w_out.shape
    size = len(offsets)
    smem = pl.BlockSpec(memory_space=pltpu.SMEM)
    vmem = pl.BlockSpec(memory_space=pltpu.VMEM)
    hbm = pl.BlockSpec(memory_space=pltpu.HBM)
    pieces = [pltpu.with_memory_space_constraint(p, pltpu.HBM) for p in pieces]
    return pl.pallas_call(
        functools.partial(attention_kernel, offsets, parts, chunk, with_base),
        in_specs=[smem, smem] + [hbm] * len(pieces) + [vmem] * 4,
        out_specs=vmem,
        out_shape=jax.ShapeDtypeStruct((size * chunk, width if with_base else local), F32 if with_base else BF),
        scratch_shapes=[pltpu.VMEM((size, chunk, width), BF), pltpu.SemaphoreType.DMA((size, parts))],
        compiler_params=pltpu.CompilerParams(vmem_limit_bytes=16 << 20),
        cost_estimate=cost(40 * size * 2 * chunk * width * 4 * local, 3 << 20),
        name="attention",
    )(me, ends, *pieces, *weights, w_out)


def first_join_kernel(context_ref, wo_ref, right_ref, left_ref):
    half = right_ref.shape[0]
    sums = dot(context_ref[...], wo_ref[...]).astype(BF)
    right_ref[...] = sums[:half]
    left_ref[...] = sums[half:]


def join_kernel(at, start, context_ref, wo_ref, recv_ref, out_ref):
    chunk, half = out_ref.shape[0], recv_ref.shape[0]
    sums = dot(context_ref[at * chunk:(at + 1) * chunk], wo_ref[...])
    rows = slice(start, start + half)
    out_ref[rows] = (sums[rows] + recv_ref[...].astype(F32)).astype(BF)
    if half < chunk:
        rest = slice(half - start, chunk - start)
        out_ref[rest] = sums[rest].astype(BF)


def middle_kernel(base_ref, right_ref, left_ref, hidden_ref, normed_ref):
    hidden = base_ref[...] + (right_ref[...].astype(F32) + left_ref[...].astype(F32))
    hidden_ref[...] = hidden
    normed_ref[...] = normalize(hidden).astype(BF)


def feed_kernel(rows_ref, *refs):
    (up_ref, down_ref, gathered_ref, out_ref, ups, downs, sems), hidden = refs[-7:], refs[:-7]
    planes = gathered_ref.shape[1]
    rows = gathered_ref.shape[2] // 2
    copies = [(pltpu.make_async_copy(up_ref, ups.at[0], sems.at[0, 0]),
               pltpu.make_async_copy(down_ref, downs.at[0], sems.at[0, 1]))]
    spread = gathered_ref.shape[0]
    for p in range(planes):
        copies.append(tuple(
            pltpu.make_async_copy(
                gathered_ref.at[:, p, t * rows:(t + 1) * rows, :],
                into.at[p + 1].reshape(spread, rows, into.shape[-1]),
                sems.at[p + 1, t],
            )
            for t, into in enumerate((ups, downs))
        ))
    for up, down in copies:
        up.start()
        down.start()
    normed = rows_ref[...]
    total = hidden[0][...] if hidden else None
    for p, (up, down) in enumerate(copies):
        up.wait()
        inner = jnp.maximum(dot(normed, ups[p]), 0.0).astype(BF)
        down.wait()
        part = dot(inner, downs[p])
        total = part if total is None else total + part
    out_ref[...] = total.astype(out_ref.dtype)


def feed(normed, hidden, w_up, w_down, gathered):
    planes = gathered.shape[1]
    count, width = normed.shape
    vmem = pl.BlockSpec(memory_space=pltpu.VMEM)
    hbm = pl.BlockSpec(memory_space=pltpu.HBM)
    w_up, w_down, gathered = (
        pltpu.with_memory_space_constraint(w, pltpu.HBM) for w in (w_up, w_down, gathered)
    )
    return pl.pallas_call(
        feed_kernel,
        in_specs=[vmem] * (1 + len(hidden)) + [hbm] * 3,
        out_specs=vmem,
        out_shape=jax.ShapeDtypeStruct(normed.shape, F32 if hidden else BF),
        scratch_shapes=[
            pltpu.VMEM((planes + 1,) + w_up.shape, BF),
            pltpu.VMEM((planes + 1,) + w_down.shape, BF),
            pltpu.SemaphoreType.DMA((planes + 1, 2)),
        ],
        compiler_params=pltpu.CompilerParams(vmem_limit_bytes=24 << 20),
        cost_estimate=cost(
            4 * count * width * w_up.shape[1] * (planes + 1), 4 * (planes + 1) * width * w_up.shape[1]
        ),
        name="feed",
    )(normed, *hidden, w_up, w_down, gathered)


def pool_kernel(hidden_ref, pair_ref, gain_ref, member_ref, length_ref, out_ref):
    hidden = hidden_ref[...] + pair_ref[...].astype(F32)
    finished = normalize(hidden) * gain_ref[...]
    pooled = dot(member_ref[...], finished, precision=HIGH) / length_ref[...]
    out_ref[...] = jnp.broadcast_to(pooled[None], out_ref.shape)


def moments_kernel(own, where_ref, pooled_ref, proj_ref, code_ref, out_ref):
    first, core = where_ref[0], where_ref[1]
    parts, few, width = pooled_ref.shape
    sentences = parts * few
    pooled = pooled_ref[...].reshape(sentences, width)
    total = out_ref.shape[0]
    per_chip = width // (total // PACK)
    mean = jnp.mean(pooled, axis=0, keepdims=True)
    large, small = split(pooled - mean)
    feature = lax.broadcasted_iota(jnp.int32, (width, total), 0)
    wanted = lax.broadcasted_iota(jnp.int32, (width, total), 1)
    chosen = (wanted // PACK) * per_chip + first + wanted % PACK
    pick = jnp.where((feature == chosen) & (wanted % PACK < own), 1.0, 0.0).astype(BF)
    picked_large, picked_small = dot(large, pick).astype(BF), dot(small, pick).astype(BF)
    rows = ((0,), (0,))
    moments = dot(picked_large, large, rows) + (dot(picked_large, small, rows) + dot(picked_small, large, rows))
    rotated = dot(large, proj_ref[...]).astype(BF)
    lanes = rotated.shape[1]
    row = lax.broadcasted_iota(jnp.int32, (total, sentences), 0)
    column = lax.broadcasted_iota(jnp.int32, (total, sentences), 1)
    target = ((row // PACK) * CORES + core) * KINDS
    half = sentences // CORES
    ones = jnp.ones((sentences, lanes), BF)
    sides = []
    for a in range(CORES):
        mine = (column // half == a) & (row % PACK == own + 2)
        there = (column // half == a) & (row % PACK == own + 3)
        for k in range(KINDS):
            hit = target + k == code_ref[...]
            sides.append(
                dot(jnp.where(mine & hit, 1.0, 0.0).astype(BF), rotated)
                + dot(jnp.where(there & hit, 1.0, 0.0).astype(BF), ones)
            )
    sides = jnp.concatenate(sides, axis=-1)
    high = mean.astype(BF).astype(F32)
    low = mean - high
    line = lax.broadcasted_iota(jnp.int32, (total, 1), 0) % PACK
    means = jnp.where(line == own, high, 0.0) + jnp.where(line == own + 1, low, 0.0)
    out_ref[...] = (moments + means + sides).astype(BF)


def combine_kernel(where_ref, recv_ref, proj_ref, pq_ref, cov_ref):
    first = where_ref[0]
    own, width = cov_ref.shape
    recv = recv_ref[...]
    total = recv.shape[0]
    chips = total // PACK
    sentences = pq_ref.shape[1]
    each = float(CORES * sentences)
    source = lax.broadcasted_iota(jnp.int32, (chips, total), 0)
    line = lax.broadcasted_iota(jnp.int32, (chips, total), 1) - source * PACK
    means = dot(jnp.where((line == own) | (line == own + 1), 1.0, 0.0).astype(BF), recv)
    sides = dot(jnp.where(line == own + 2, 1.0, 0.0).astype(BF), recv).astype(BF)
    there = dot(jnp.where(line == own + 3, 1.0, 0.0).astype(BF), recv).astype(BF)
    line = lax.broadcasted_iota(jnp.int32, (PACK, total), 1) % PACK
    within = dot(jnp.where(line == lax.broadcasted_iota(jnp.int32, (PACK, total), 0), 1.0, 0.0).astype(BF), recv)
    away = means - jnp.mean(means, axis=0, keepdims=True)
    feature = lax.broadcasted_iota(jnp.int32, (width, LANES), 0)
    lane = lax.broadcasted_iota(jnp.int32, (width, LANES), 1)
    pick = jnp.where((feature == first + lane) & (lane < own), 1.0, 0.0).astype(BF)
    large, small = split(away)
    picked_large, picked_small = dot(large, pick).astype(BF), dot(small, pick).astype(BF)
    rows = ((0,), (0,))
    between = dot(picked_large, large, rows) + (dot(picked_large, small, rows) + dot(picked_small, large, rows))
    cov_ref[...] = (within[:own] + each * between[:own]) / (each * float(chips))
    shift = dot(large, proj_ref[...]) + dot(small, proj_ref[...])
    shift_large, shift_small = split(shift)
    lanes = shift.shape[1]
    one = lax.broadcasted_iota(jnp.int32, (chips, chips), 0)
    other = lax.broadcasted_iota(jnp.int32, (chips, chips), 1)
    ahead = jnp.where(one < other, 1.0, 0.0).astype(BF)
    same = jnp.where(one == other, 1.0, 0.0).astype(BF)
    kinds = [a * KINDS + 2 * c for a in range(CORES) for c in range(SLOTS)]
    filled = [there[:, k * lanes:(k + 1) * lanes] for k in kinds]
    flat = [dot(f, same, ((0,), (0,)))[:1] for f in filled]
    before = sum(dot(f, ahead, ((0,), (0,)))[:1] for f in filled)
    place = lax.broadcasted_iota(jnp.int32, (sentences, chips), 0)
    result = jnp.zeros((sentences, lanes), F32)
    for kind, here in zip(kinds, flat):
        for k in range(2):
            position = (2.0 * before + float(k)).astype(jnp.int32)
            chosen = jnp.where((place == position) & (here > 0.5), 1.0, 0.0).astype(BF)
            block = sides[:, (kind + k) * lanes:(kind + k + 1) * lanes]
            result = result + (dot(chosen, block) + (dot(chosen, shift_large) + dot(chosen, shift_small)))
        before = before + here
    for q in range(pq_ref.shape[0]):
        pq_ref[q] = result[:, q * SUBW:(q + 1) * SUBW]


def small_call(kernel, outs, args, scalar=None, name=None):
    specs = [pl.BlockSpec(memory_space=pltpu.VMEM) for _ in args]
    if scalar is not None:
        specs = [pl.BlockSpec(memory_space=pltpu.SMEM)] + specs
        args = (scalar,) + tuple(args)
    single = not isinstance(outs, (tuple, list))
    return pl.pallas_call(
        kernel,
        in_specs=specs,
        out_specs=pl.BlockSpec(memory_space=pltpu.VMEM) if single else [pl.BlockSpec(memory_space=pltpu.VMEM) for _ in outs],
        out_shape=outs,
        compiler_params=pltpu.CompilerParams(vmem_limit_bytes=16 << 20),
        cost_estimate=cost(1 << 20, 1 << 20),
        name=name,
    )(*args)


def on_device(
    tokens, lengths, dest, w_query, w_key, w_value, w_out, w_up, w_down, final_gain, projection
):
    dp_count = lax.axis_size("dp")
    sub_count = lax.axis_size("sub")
    dp_at = lax.axis_index("dp")
    sub_at = lax.axis_index("sub")
    block_count, per_block = lengths.shape
    local_rows, local_width = tokens.shape
    block_rows = local_rows // block_count
    width = local_width * sub_count
    own_blocks = block_count // sub_count
    own_rows = own_blocks * block_rows
    half = sub_count // 2

    def move(array, by):
        return lax.ppermute(array, "sub", [(i, (i + by) % sub_count) for i in range(sub_count)])

    def swap(array):
        return lax.ppermute(array, "sub", [(i, i ^ 1) for i in range(sub_count)])

    rows = w_up.shape[0] // dp_count
    piece = jnp.concatenate(
        [lax.dynamic_slice_in_dim(w, dp_at * rows, rows, 0) for w in (w_up, w_down)], axis=0
    )
    piece, tokens = lax.optimization_barrier((piece, tokens))
    across = lax.ppermute(
        piece, "sub", [(i, (i + (half - 1 if i % 2 else 1 - half)) % sub_count) for i in range(sub_count)]
    )
    others = [move(piece, 2), move(piece, -2), across]
    planes = len(others)

    ends = jnp.cumsum(lengths, axis=-1)
    position = jnp.arange(block_rows, dtype=jnp.int32)
    segment = jnp.sum((ends[:, None, :] <= position[None, :, None]).astype(jnp.int32), axis=-1)
    ordinal = jnp.arange(block_count, dtype=jnp.int32)
    keys = (ordinal[:, None] * per_block + segment).reshape(local_rows)
    own_lens = lax.dynamic_slice_in_dim(lengths, sub_at * own_blocks, own_blocks, 0)
    own_keys = lax.dynamic_slice_in_dim(keys, sub_at * own_rows, own_rows, 0)
    own_sentences = own_blocks * per_block
    member = (
        own_keys[None, :] == sub_at * own_sentences + jnp.arange(own_sentences, dtype=jnp.int32)[:, None]
    ).astype(F32)
    matches = dest[:, None] == dest[None, :]
    earlier = ordinal[:, None] > ordinal[None, :]
    earlier_count = jnp.sum((matches & earlier).astype(jnp.int32), axis=1)
    code = (dest * SLOTS + earlier_count)[:, None] * per_block + jnp.arange(per_block, dtype=jnp.int32)[None, :]
    code = code.reshape(1, block_count * per_block)
    chips = dp_count // CORES
    siblings = [[q * CORES + c for c in range(CORES)] for q in range(chips)]
    other = lax.ppermute(code, "dp", [(i, i ^ 1) for i in range(dp_count)])
    core = dp_at % CORES
    code = jnp.where(core == 0, jnp.concatenate((code, other), axis=1), jnp.concatenate((other, code), axis=1))
    columns = width // sub_count
    proj = lax.dynamic_slice_in_dim(projection, sub_at * columns, columns, 1)

    behind, ahead = [], []
    right = left = tokens
    for step in range(half - 1):
        right, left = move(right, 1), move(left, -1)
        if step == 0:
            others = lax.optimization_barrier((others, right, left))[0]
        behind.append(right)
        ahead.append(left)
    halfway = local_rows // 2
    far = [move(right[:halfway], 1), move(left[halfway:], -1)]
    pieces = [tokens] + ahead + far + behind

    gathered = lax.all_gather(jnp.concatenate(others, axis=0), "dp", axis=0, tiled=True)
    gathered = gathered.reshape(dp_count, planes, 2 * rows, width)

    attend = functools.partial(attention, pieces, (w_query, w_key, w_value), w_out, lengths.T, sub_at.reshape(1))
    own_shape = (own_rows, width)
    half_shape = (own_rows // 2, width)
    right, left = small_call(
        first_join_kernel,
        [jax.ShapeDtypeStruct(half_shape, BF)] * 2,
        (attend([half]), w_out),
        name="join",
    )
    right, left = move(right, 1), move(left, -1)
    for away in range(half - 1, 0, -1):
        context = attend([away, -away])
        join = lambda at, start, recv: small_call(
            functools.partial(join_kernel, at, start),
            jax.ShapeDtypeStruct(own_shape, BF),
            (context, w_out, recv),
            name="join",
        )
        right, left = move(join(0, 0, right), 1), move(join(1, own_rows - left.shape[0], left), -1)
    base = attend([0], with_base=True)
    hidden1, normed2 = small_call(
        middle_kernel,
        (jax.ShapeDtypeStruct(own_shape, F32), jax.ShapeDtypeStruct(own_shape, BF)),
        (base, right, left),
        name="middle",
    )
    sent = feed(swap(normed2), (), w_up, w_down, gathered)
    hidden2 = feed(normed2, (hidden1,), w_up, w_down, gathered)
    pooled = small_call(
        pool_kernel,
        jax.ShapeDtypeStruct((sub_count, own_sentences, width), F32),
        (hidden2, swap(sent), final_gain[None, :], member, own_lens.reshape(own_sentences, 1).astype(F32)),
        name="pool",
    )
    pooled = lax.all_to_all(pooled, "sub", split_axis=0, concat_axis=0, tiled=True)
    pooled = lax.all_gather(pooled, "dp", axis=0, tiled=True, axis_index_groups=siblings)
    sentences = sub_count * own_sentences
    cov_rows = width // (dp_count * sub_count)
    sent = small_call(
        functools.partial(moments_kernel, cov_rows),
        jax.ShapeDtypeStruct((chips * PACK, width), BF),
        (pooled, proj, code),
        scalar=jnp.stack([(core * sub_count + sub_at) * cov_rows, core]).astype(jnp.int32),
        name="moments",
    )
    received = lax.all_to_all(
        sent.reshape(chips, PACK, width), "dp", split_axis=0, concat_axis=0, tiled=True,
        axis_index_groups=[[q * CORES + c for q in range(chips)] for c in range(CORES)],
    ).reshape(chips * PACK, width)
    return small_call(
        combine_kernel,
        (
            jax.ShapeDtypeStruct((columns // SUBW, sentences, SUBW), F32),
            jax.ShapeDtypeStruct((cov_rows, width), F32),
        ),
        (received, proj),
        scalar=((dp_at * sub_count + sub_at) * cov_rows).reshape(1),
        name="combine",
    )


def solution(mesh):
    in_specs = (
        P("dp", "sub"),
        P("dp", None),
        P("dp"),
        P(None, "sub"),
        P(None, "sub"),
        P(None, "sub"),
        P("sub", None),
        P(None, "sub"),
        P("sub", None),
        P(),
        P(),
    )
    out_specs = (P("sub", "dp", None), P(("dp", "sub"), None))
    return jax.shard_map(
        on_device, mesh=mesh, in_specs=in_specs, out_specs=out_specs, check_vma=False
    )
```

```python
import functools
import math

import jax
import jax.numpy as jnp
from jax import lax
from jax.experimental import pallas as pl
from jax.experimental.pallas import tpu as pltpu
from jax.sharding import PartitionSpec as P

HDIM = 64
SUBW = 64
LANES = 128
SLOTS = 2
CORES = 2
KINDS = 4
PACK = 8

epsilon = 1e-05
BF = jnp.bfloat16
F32 = jnp.float32
HIGH = lax.Precision.HIGHEST


def normalize(rows):
    center = jnp.mean(rows, axis=-1, keepdims=True)
    shifted = rows - center
    spread = jnp.mean(shifted * shifted, axis=-1, keepdims=True)
    return shifted * lax.rsqrt(spread + epsilon)


def dot(a, b, dims=((1,), (0,)), precision=None):
    return lax.dot_general(a, b, (dims, ((), ())), precision=precision, preferred_element_type=F32)


def split(array):
    high = array.astype(BF)
    return high, (array - high.astype(F32)).astype(BF)


def cost(flops, size):
    return pl.CostEstimate(flops=flops, bytes_accessed=size, transcendentals=0)


def attention_kernel(offsets, parts, chunk, with_base, me_ref, ends_ref, *refs):
    pieces, (wq_ref, wk_ref, wv_ref, wo_ref), rest = refs[:parts + 1], refs[parts + 1:parts + 5], refs[parts + 5:]
    out_ref, rows_ref, sems = rest
    me = me_ref[0]
    half = parts // 2
    part = pieces[0].shape[1]
    chunks = [lax.rem(me + (off + parts), parts) for off in offsets]

    def slot(i, away):
        at = lax.rem(me + (away + parts), parts)
        return rows_ref.at[i, :, pl.ds(pl.multiple_of(at * part, part), part)]

    def fetch(source, start, i, away, number):
        start = pl.multiple_of(start, chunk)
        return pltpu.make_async_copy(source.at[pl.ds(start, chunk), :], slot(i, away), sems.at[i, number])

    for i, c in enumerate(chunks):
        for k in range(half):
            fetch(pieces[k], c * chunk, i, k, k).start()
        for k in range(1, half):
            fetch(pieces[half + 1 + k], c * chunk, i, -k, half + k).start()

        @pl.when(c < half)
        def _():
            fetch(pieces[half], c * chunk, i, half, half).start()

        @pl.when(c >= half)
        def _():
            fetch(pieces[half + 1], (c - half) * chunk, i, half, half).start()

    for i, c in enumerate(chunks):
        for k in range(half):
            fetch(pieces[k], c * chunk, i, k, k).wait()
        for k in range(1, half):
            fetch(pieces[half + 1 + k], c * chunk, i, -k, half + k).wait()
        fetch(pieces[half], 0, i, half, half).wait()
    count = len(offsets)
    rows = rows_ref[...].reshape(count * chunk, -1).astype(F32)
    normed = normalize(rows).astype(BF)
    w_qkv = jnp.concatenate([wq_ref[...], wk_ref[...], wv_ref[...]], axis=1)
    projected = dot(normed, w_qkv).astype(BF)
    local = wo_ref.shape[0]
    block_rows = chunk * parts // ends_ref.shape[1]
    blocks = chunk // block_rows
    per_block = ends_ref.shape[0]

    def keys(c, shape, axis):
        row = lax.broadcasted_iota(jnp.int32, shape, axis)
        block = row // block_rows
        key = block * per_block
        for b in range(blocks):
            end = b * block_rows
            for e in range(per_block - 1):
                end = end + ends_ref[e, c * blocks + b]
                key = key + jnp.where((block == b) & (row >= end), 1, 0)
        return key

    lines = []
    for i, c in enumerate(chunks):
        mine = projected[i * chunk:(i + 1) * chunk]
        matches = keys(c, (chunk, 1), 0) == keys(c, (1, chunk), 1)
        heads = []
        for h in range(local // HDIM):
            query, key, value = (
                mine[:, t * local + h * HDIM:t * local + (h + 1) * HDIM] for t in range(3)
            )
            scores = dot(query, key, ((1,), (1,))) / math.sqrt(HDIM)
            raised = jnp.where(matches, jnp.exp(scores), 0.0)
            weights = (raised / jnp.sum(raised, axis=-1, keepdims=True)).astype(BF)
            heads.append(dot(weights, value).astype(BF))
        lines.append(jnp.concatenate(heads, axis=-1))
    context = jnp.concatenate(lines, axis=0)
    if with_base:
        out_ref[...] = rows + dot(context, wo_ref[...])
    else:
        out_ref[...] = context


def attention(pieces, weights, w_out, ends, me, offsets, with_base=False):
    parts = len(pieces) - 1
    count, part = pieces[0].shape
    chunk = count // parts
    local, width = w_out.shape
    size = len(offsets)
    smem = pl.BlockSpec(memory_space=pltpu.SMEM)
    vmem = pl.BlockSpec(memory_space=pltpu.VMEM)
    hbm = pl.BlockSpec(memory_space=pltpu.HBM)
    pieces = [pltpu.with_memory_space_constraint(p, pltpu.HBM) for p in pieces]
    return pl.pallas_call(
        functools.partial(attention_kernel, offsets, parts, chunk, with_base),
        in_specs=[smem, smem] + [hbm] * len(pieces) + [vmem] * 4,
        out_specs=vmem,
        out_shape=jax.ShapeDtypeStruct((size * chunk, width if with_base else local), F32 if with_base else BF),
        scratch_shapes=[pltpu.VMEM((size, chunk, width), BF), pltpu.SemaphoreType.DMA((size, parts))],
        compiler_params=pltpu.CompilerParams(vmem_limit_bytes=16 << 20),
        cost_estimate=cost(40 * size * 2 * chunk * width * 4 * local, 3 << 20),
        name="attention",
    )(me, ends, *pieces, *weights, w_out)


def first_join_kernel(context_ref, wo_ref, right_ref, left_ref):
    half = right_ref.shape[0]
    sums = dot(context_ref[...], wo_ref[...]).astype(BF)
    right_ref[...] = sums[:half]
    left_ref[...] = sums[half:]


def join_kernel(at, start, context_ref, wo_ref, recv_ref, out_ref):
    chunk, half = out_ref.shape[0], recv_ref.shape[0]
    sums = dot(context_ref[at * chunk:(at + 1) * chunk], wo_ref[...])
    rows = slice(start, start + half)
    out_ref[rows] = (sums[rows] + recv_ref[...].astype(F32)).astype(BF)
    if half < chunk:
        rest = slice(half - start, chunk - start)
        out_ref[rest] = sums[rest].astype(BF)


def middle_kernel(base_ref, right_ref, left_ref, hidden_ref, normed_ref):
    hidden = base_ref[...] + (right_ref[...].astype(F32) + left_ref[...].astype(F32))
    hidden_ref[...] = hidden
    normed_ref[...] = normalize(hidden).astype(BF)


def feed_kernel(rows_ref, *refs):
    (up_ref, down_ref, gathered_ref, out_ref, ups, downs, sems), hidden = refs[-7:], refs[:-7]
    planes = gathered_ref.shape[1]
    rows = gathered_ref.shape[2] // 2
    copies = [(pltpu.make_async_copy(up_ref, ups.at[0], sems.at[0, 0]),
               pltpu.make_async_copy(down_ref, downs.at[0], sems.at[0, 1]))]
    spread = gathered_ref.shape[0]
    for p in range(planes):
        copies.append(tuple(
            pltpu.make_async_copy(
                gathered_ref.at[:, p, t * rows:(t + 1) * rows, :],
                into.at[p + 1].reshape(spread, rows, into.shape[-1]),
                sems.at[p + 1, t],
            )
            for t, into in enumerate((ups, downs))
        ))
    for up, down in copies:
        up.start()
        down.start()
    normed = rows_ref[...]
    total = hidden[0][...] if hidden else None
    for p, (up, down) in enumerate(copies):
        up.wait()
        inner = jnp.maximum(dot(normed, ups[p]), 0.0).astype(BF)
        down.wait()
        part = dot(inner, downs[p])
        total = part if total is None else total + part
    out_ref[...] = total.astype(out_ref.dtype)


def feed(normed, hidden, w_up, w_down, gathered):
    planes = gathered.shape[1]
    count, width = normed.shape
    vmem = pl.BlockSpec(memory_space=pltpu.VMEM)
    hbm = pl.BlockSpec(memory_space=pltpu.HBM)
    w_up, w_down, gathered = (
        pltpu.with_memory_space_constraint(w, pltpu.HBM) for w in (w_up, w_down, gathered)
    )
    return pl.pallas_call(
        feed_kernel,
        in_specs=[vmem] * (1 + len(hidden)) + [hbm] * 3,
        out_specs=vmem,
        out_shape=jax.ShapeDtypeStruct(normed.shape, F32 if hidden else BF),
        scratch_shapes=[
            pltpu.VMEM((planes + 1,) + w_up.shape, BF),
            pltpu.VMEM((planes + 1,) + w_down.shape, BF),
            pltpu.SemaphoreType.DMA((planes + 1, 2)),
        ],
        compiler_params=pltpu.CompilerParams(vmem_limit_bytes=24 << 20),
        cost_estimate=cost(
            4 * count * width * w_up.shape[1] * (planes + 1), 4 * (planes + 1) * width * w_up.shape[1]
        ),
        name="feed",
    )(normed, *hidden, w_up, w_down, gathered)


def pool_kernel(hidden_ref, pair_ref, gain_ref, member_ref, length_ref, out_ref):
    hidden = hidden_ref[...] + pair_ref[...].astype(F32)
    finished = normalize(hidden) * gain_ref[...]
    pooled = dot(member_ref[...], finished, precision=HIGH) / length_ref[...]
    out_ref[...] = jnp.broadcast_to(pooled[None], out_ref.shape)


def moments_kernel(own, where_ref, pooled_ref, proj_ref, code_ref, out_ref):
    first, core = where_ref[0], where_ref[1]
    parts, few, width = pooled_ref.shape
    sentences = parts * few
    pooled = pooled_ref[...].reshape(sentences, width)
    total = out_ref.shape[0]
    per_chip = width // (total // PACK)
    mean = jnp.mean(pooled, axis=0, keepdims=True)
    large, small = split(pooled - mean)
    feature = lax.broadcasted_iota(jnp.int32, (width, total), 0)
    wanted = lax.broadcasted_iota(jnp.int32, (1, total), 1)
    chosen = jnp.where(wanted % PACK < own, (wanted // PACK) * per_chip + first + wanted % PACK, -1)
    pick = jnp.where(feature == chosen, 1.0, 0.0).astype(BF)
    picked_large, picked_small = dot(large, pick).astype(BF), dot(small, pick).astype(BF)
    rows = ((0,), (0,))
    moments = dot(picked_large, large, rows) + (dot(picked_large, small, rows) + dot(picked_small, large, rows))
    rotated = dot(large, proj_ref[...]).astype(BF)
    lanes = rotated.shape[1]
    chips = total // PACK
    row = lax.broadcasted_iota(jnp.int32, (CORES * KINDS * chips, 1), 0)
    column = lax.broadcasted_iota(jnp.int32, (1, sentences), 1)
    kind = row // chips
    target = ((row % chips) * CORES + core) * KINDS + kind % KINDS
    hit = (target == code_ref[...]) & (column // (sentences // CORES) == kind // KINDS)
    place = jnp.where(hit, 1.0, 0.0)
    there = jnp.broadcast_to(jnp.sum(place, axis=1, keepdims=True), (place.shape[0], lanes))
    wide = [
        jnp.concatenate([part[k * chips:(k + 1) * chips] for k in range(CORES * KINDS)], axis=-1)
        for part in (dot(place.astype(BF), rotated), there)
    ]
    row = lax.broadcasted_iota(jnp.int32, (total, 1), 0)
    column = lax.broadcasted_iota(jnp.int32, (1, CORES * chips), 1)
    spread = (row // PACK == column % chips) & (row % PACK == own + 2 + column // chips)
    sides = dot(jnp.where(spread, 1.0, 0.0).astype(BF), jnp.concatenate(wide, axis=0).astype(BF))
    high = mean.astype(BF).astype(F32)
    low = mean - high
    line = lax.broadcasted_iota(jnp.int32, (total, 1), 0) % PACK
    means = jnp.where(line == own, high, 0.0) + jnp.where(line == own + 1, low, 0.0)
    out_ref[...] = (moments + means + sides).astype(BF)


def combine_kernel(where_ref, recv_ref, proj_ref, pq_ref, cov_ref):
    first = where_ref[0]
    own, width = cov_ref.shape
    recv = recv_ref[...]
    total = recv.shape[0]
    chips = total // PACK
    sentences = pq_ref.shape[1]
    each = float(CORES * sentences)
    row = lax.broadcasted_iota(jnp.int32, (3 * chips + PACK, 1), 0)
    line = lax.broadcasted_iota(jnp.int32, (1, total), 1)
    kind, source = row // chips, row % chips
    away = line - source * PACK
    taken = (kind == 0) & ((away == own) | (away == own + 1))
    taken = taken | ((kind == 1) & (away == own + 2)) | ((kind == 2) & (away == own + 3))
    taken = taken | ((kind == 3) & (line % PACK == source))
    parts = dot(jnp.where(taken, 1.0, 0.0).astype(BF), recv)
    means = parts[:chips]
    sides = parts[chips:2 * chips].astype(BF)
    there = parts[2 * chips:3 * chips].astype(BF)
    within = parts[3 * chips:]
    away = means - jnp.mean(means, axis=0, keepdims=True)
    feature = lax.broadcasted_iota(jnp.int32, (width, LANES), 0)
    lane = lax.broadcasted_iota(jnp.int32, (1, LANES), 1)
    pick = jnp.where(feature == jnp.where(lane < own, first + lane, -1), 1.0, 0.0).astype(BF)
    large, small = split(away)
    picked_large, picked_small = dot(large, pick).astype(BF), dot(small, pick).astype(BF)
    rows = ((0,), (0,))
    between = dot(picked_large, large, rows) + (dot(picked_large, small, rows) + dot(picked_small, large, rows))
    cov_ref[...] = (within[:own] + each * between[:own]) / (each * float(chips))
    shift = dot(large, proj_ref[...]) + dot(small, proj_ref[...])
    shift_large, shift_small = split(shift)
    lanes = shift.shape[1]
    kinds = CORES * KINDS
    stack = lambda wide: jnp.concatenate([wide[:, k * lanes:(k + 1) * lanes] for k in range(kinds)], axis=0)
    size = kinds * chips
    one = lax.broadcasted_iota(jnp.int32, (size, 1), 0)
    other = lax.broadcasted_iota(jnp.int32, (1, size), 1)
    one_kind, one_chip, other_kind, other_chip = one // chips, one % chips, other // chips, other % chips
    ahead = (one_chip < other_chip) | ((one_chip == other_chip) & (one_kind // 2 < other_kind // 2))
    ahead = jnp.where(ahead & (one_kind % 2 == 0), 1.0, 0.0).astype(BF)
    same = jnp.where(one == other, 1.0, 0.0).astype(BF)
    flags = stack(there)[:, :8]
    before = dot(flags, ahead, ((0,), (0,)))[:1]
    here = dot(flags, same, ((0,), (0,)))[:1]
    place = lax.broadcasted_iota(jnp.int32, (sentences, size), 0)
    odd = (lax.broadcasted_iota(jnp.int32, (1, size), 1) // chips) % 2
    position = 2 * before.astype(jnp.int32) + odd
    chosen = jnp.where((place == position) & (here > 0.5), 1.0, 0.0).astype(BF)
    tiled = lambda array: jnp.concatenate([array] * kinds, axis=0)
    result = dot(chosen, stack(sides)) + (dot(chosen, tiled(shift_large)) + dot(chosen, tiled(shift_small)))
    for q in range(pq_ref.shape[0]):
        pq_ref[q] = result[:, q * SUBW:(q + 1) * SUBW]


def small_call(kernel, outs, args, scalar=None, name=None):
    specs = [pl.BlockSpec(memory_space=pltpu.VMEM) for _ in args]
    if scalar is not None:
        specs = [pl.BlockSpec(memory_space=pltpu.SMEM)] + specs
        args = (scalar,) + tuple(args)
    single = not isinstance(outs, (tuple, list))
    return pl.pallas_call(
        kernel,
        in_specs=specs,
        out_specs=pl.BlockSpec(memory_space=pltpu.VMEM) if single else [pl.BlockSpec(memory_space=pltpu.VMEM) for _ in outs],
        out_shape=outs,
        compiler_params=pltpu.CompilerParams(vmem_limit_bytes=16 << 20),
        cost_estimate=cost(1 << 20, 1 << 20),
        name=name,
    )(*args)


def on_device(
    tokens, lengths, dest, w_query, w_key, w_value, w_out, w_up, w_down, final_gain, projection
):
    dp_count = lax.axis_size("dp")
    sub_count = lax.axis_size("sub")
    dp_at = lax.axis_index("dp")
    sub_at = lax.axis_index("sub")
    block_count, per_block = lengths.shape
    local_rows, local_width = tokens.shape
    block_rows = local_rows // block_count
    width = local_width * sub_count
    own_blocks = block_count // sub_count
    own_rows = own_blocks * block_rows
    half = sub_count // 2

    def move(array, by):
        return lax.ppermute(array, "sub", [(i, (i + by) % sub_count) for i in range(sub_count)])

    def swap(array):
        return lax.ppermute(array, "sub", [(i, i ^ 1) for i in range(sub_count)])

    rows = w_up.shape[0] // dp_count
    piece = jnp.concatenate(
        [lax.dynamic_slice_in_dim(w, dp_at * rows, rows, 0) for w in (w_up, w_down)], axis=0
    )
    across = lax.ppermute(
        piece, "sub", [(i, (i + (half - 1 if i % 2 else 1 - half)) % sub_count) for i in range(sub_count)]
    )
    others = [move(piece, 2), move(piece, -2), across]
    planes = len(others)

    ends = jnp.cumsum(lengths, axis=-1)
    position = jnp.arange(block_rows, dtype=jnp.int32)
    segment = jnp.sum((ends[:, None, :] <= position[None, :, None]).astype(jnp.int32), axis=-1)
    ordinal = jnp.arange(block_count, dtype=jnp.int32)
    keys = (ordinal[:, None] * per_block + segment).reshape(local_rows)
    own_lens = lax.dynamic_slice_in_dim(lengths, sub_at * own_blocks, own_blocks, 0)
    own_keys = lax.dynamic_slice_in_dim(keys, sub_at * own_rows, own_rows, 0)
    own_sentences = own_blocks * per_block
    member = (
        own_keys[None, :] == sub_at * own_sentences + jnp.arange(own_sentences, dtype=jnp.int32)[:, None]
    ).astype(F32)
    matches = dest[:, None] == dest[None, :]
    earlier = ordinal[:, None] > ordinal[None, :]
    earlier_count = jnp.sum((matches & earlier).astype(jnp.int32), axis=1)
    code = (dest * SLOTS + earlier_count)[:, None] * per_block + jnp.arange(per_block, dtype=jnp.int32)[None, :]
    code = code.reshape(1, block_count * per_block)
    chips = dp_count // CORES
    siblings = [[q * CORES + c for c in range(CORES)] for q in range(chips)]
    other = lax.ppermute(code, "dp", [(i, i ^ 1) for i in range(dp_count)])
    core = dp_at % CORES
    code = jnp.where(core == 0, jnp.concatenate((code, other), axis=1), jnp.concatenate((other, code), axis=1))
    columns = width // sub_count
    proj = lax.dynamic_slice_in_dim(projection, sub_at * columns, columns, 1)

    behind, ahead = [], []
    right = left = tokens
    for step in range(half - 1):
        right, left = move(right, 1), move(left, -1)
        if step == 0:
            others = lax.optimization_barrier((others, right, left))[0]
        behind.append(right)
        ahead.append(left)
    halfway = local_rows // 2
    far = [move(right[:halfway], 1), move(left[halfway:], -1)]
    pieces = [tokens] + ahead + far + behind

    gathered = lax.all_gather(jnp.concatenate(others, axis=0), "dp", axis=0, tiled=True)
    gathered = gathered.reshape(dp_count, planes, 2 * rows, width)

    attend = functools.partial(attention, pieces, (w_query, w_key, w_value), w_out, lengths.T, sub_at.reshape(1))
    own_shape = (own_rows, width)
    half_shape = (own_rows // 2, width)
    right, left = small_call(
        first_join_kernel,
        [jax.ShapeDtypeStruct(half_shape, BF)] * 2,
        (attend([half]), w_out),
        name="join",
    )
    right, left = move(right, 1), move(left, -1)
    for away in range(half - 1, 0, -1):
        context = attend([away, -away])
        join = lambda at, start, recv: small_call(
            functools.partial(join_kernel, at, start),
            jax.ShapeDtypeStruct(own_shape, BF),
            (context, w_out, recv),
            name="join",
        )
        right, left = move(join(0, 0, right), 1), move(join(1, own_rows - left.shape[0], left), -1)
    base = attend([0], with_base=True)
    hidden1, normed2 = small_call(
        middle_kernel,
        (jax.ShapeDtypeStruct(own_shape, F32), jax.ShapeDtypeStruct(own_shape, BF)),
        (base, right, left),
        name="middle",
    )
    sent = feed(swap(normed2), (), w_up, w_down, gathered)
    hidden2 = feed(normed2, (hidden1,), w_up, w_down, gathered)
    pooled = small_call(
        pool_kernel,
        jax.ShapeDtypeStruct((sub_count, own_sentences, width), F32),
        (hidden2, swap(sent), final_gain[None, :], member, own_lens.reshape(own_sentences, 1).astype(F32)),
        name="pool",
    )
    pooled = lax.all_to_all(pooled, "sub", split_axis=0, concat_axis=0, tiled=True)
    pooled = lax.all_gather(pooled, "dp", axis=0, tiled=True, axis_index_groups=siblings)
    sentences = sub_count * own_sentences
    cov_rows = width // (dp_count * sub_count)
    sent = small_call(
        functools.partial(moments_kernel, cov_rows),
        jax.ShapeDtypeStruct((chips * PACK, width), BF),
        (pooled, proj, code),
        scalar=jnp.stack([(core * sub_count + sub_at) * cov_rows, core]).astype(jnp.int32),
        name="moments",
    )
    received = lax.all_to_all(
        sent.reshape(chips, PACK, width), "dp", split_axis=0, concat_axis=0, tiled=True,
        axis_index_groups=[[q * CORES + c for q in range(chips)] for c in range(CORES)],
    ).reshape(chips * PACK, width)
    return small_call(
        combine_kernel,
        (
            jax.ShapeDtypeStruct((columns // SUBW, sentences, SUBW), F32),
            jax.ShapeDtypeStruct((cov_rows, width), F32),
        ),
        (received, proj),
        scalar=((dp_at * sub_count + sub_at) * cov_rows).reshape(1),
        name="combine",
    )


def solution(mesh):
    in_specs = (
        P("dp", "sub"),
        P("dp", None),
        P("dp"),
        P(None, "sub"),
        P(None, "sub"),
        P(None, "sub"),
        P("sub", None),
        P(None, "sub"),
        P("sub", None),
        P(),
        P(),
    )
    out_specs = (P("sub", "dp", None), P(("dp", "sub"), None))
    return jax.shard_map(
        on_device, mesh=mesh, in_specs=in_specs, out_specs=out_specs, check_vma=False
    )
```

```python
import functools
import math

import jax
import jax.numpy as jnp
from jax import lax
from jax.experimental import pallas as pl
from jax.experimental.pallas import tpu as pltpu
from jax.sharding import PartitionSpec as P

HDIM = 64
SUBW = 64
LANES = 128
SLOTS = 2
CORES = 2
KINDS = 4
PACK = 8

epsilon = 1e-05
BF = jnp.bfloat16
F32 = jnp.float32
HIGH = lax.Precision.HIGHEST


def normalize(rows):
    center = jnp.mean(rows, axis=-1, keepdims=True)
    shifted = rows - center
    spread = jnp.mean(shifted * shifted, axis=-1, keepdims=True)
    return shifted * lax.rsqrt(spread + epsilon)


def dot(a, b, dims=((1,), (0,)), precision=None):
    return lax.dot_general(a, b, (dims, ((), ())), precision=precision, preferred_element_type=F32)


def split(array):
    high = array.astype(BF)
    return high, (array - high.astype(F32)).astype(BF)


def cost(flops, size):
    return pl.CostEstimate(flops=flops, bytes_accessed=size, transcendentals=0)


def attention_kernel(offsets, parts, chunk, with_base, me_ref, ends_ref, *refs):
    pieces, (wq_ref, wk_ref, wv_ref, wo_ref), rest = refs[:parts + 1], refs[parts + 1:parts + 5], refs[parts + 5:]
    out_ref, rows_ref, sems = rest
    me = me_ref[0]
    half = parts // 2
    part = pieces[0].shape[1]
    chunks = [lax.rem(me + (off + parts), parts) for off in offsets]

    def slot(i, away):
        at = lax.rem(me + (away + parts), parts)
        return rows_ref.at[i, :, pl.ds(pl.multiple_of(at * part, part), part)]

    def fetch(source, start, i, away, number):
        start = pl.multiple_of(start, chunk)
        return pltpu.make_async_copy(source.at[pl.ds(start, chunk), :], slot(i, away), sems.at[i, number])

    for i, c in enumerate(chunks):
        for k in range(half):
            fetch(pieces[k], c * chunk, i, k, k).start()
        for k in range(1, half):
            fetch(pieces[half + 1 + k], c * chunk, i, -k, half + k).start()

        @pl.when(c < half)
        def _():
            fetch(pieces[half], c * chunk, i, half, half).start()

        @pl.when(c >= half)
        def _():
            fetch(pieces[half + 1], (c - half) * chunk, i, half, half).start()

    for i, c in enumerate(chunks):
        for k in range(half):
            fetch(pieces[k], c * chunk, i, k, k).wait()
        for k in range(1, half):
            fetch(pieces[half + 1 + k], c * chunk, i, -k, half + k).wait()
        fetch(pieces[half], 0, i, half, half).wait()
    count = len(offsets)
    rows = rows_ref[...].reshape(count * chunk, -1).astype(F32)
    normed = normalize(rows).astype(BF)
    w_qkv = jnp.concatenate([wq_ref[...], wk_ref[...], wv_ref[...]], axis=1)
    projected = dot(normed, w_qkv).astype(BF)
    local = wo_ref.shape[0]
    block_rows = chunk * parts // ends_ref.shape[1]
    blocks = chunk // block_rows
    per_block = ends_ref.shape[0]

    def keys(c, shape, axis):
        row = lax.broadcasted_iota(jnp.int32, shape, axis)
        block = row // block_rows
        key = block * per_block
        for b in range(blocks):
            end = b * block_rows
            for e in range(per_block - 1):
                end = end + ends_ref[e, c * blocks + b]
                key = key + jnp.where((block == b) & (row >= end), 1, 0)
        return key

    lines = []
    for i, c in enumerate(chunks):
        mine = projected[i * chunk:(i + 1) * chunk]
        matches = keys(c, (chunk, 1), 0) == keys(c, (1, chunk), 1)
        heads = []
        for h in range(local // HDIM):
            query, key, value = (
                mine[:, t * local + h * HDIM:t * local + (h + 1) * HDIM] for t in range(3)
            )
            scores = dot(query, key, ((1,), (1,))) / math.sqrt(HDIM)
            raised = jnp.where(matches, jnp.exp(scores), 0.0)
            weights = (raised / jnp.sum(raised, axis=-1, keepdims=True)).astype(BF)
            heads.append(dot(weights, value).astype(BF))
        lines.append(jnp.concatenate(heads, axis=-1))
    context = jnp.concatenate(lines, axis=0)
    if with_base:
        out_ref[...] = rows + dot(context, wo_ref[...])
    else:
        out_ref[...] = context


def attention(pieces, weights, w_out, ends, me, offsets, with_base=False):
    parts = len(pieces) - 1
    count, part = pieces[0].shape
    chunk = count // parts
    local, width = w_out.shape
    size = len(offsets)
    smem = pl.BlockSpec(memory_space=pltpu.SMEM)
    vmem = pl.BlockSpec(memory_space=pltpu.VMEM)
    hbm = pl.BlockSpec(memory_space=pltpu.HBM)
    half = parts // 2
    pieces = [
        p if k in (half, half + 1) else pltpu.with_memory_space_constraint(p, pltpu.HBM) for k, p in enumerate(pieces)
    ]
    return pl.pallas_call(
        functools.partial(attention_kernel, offsets, parts, chunk, with_base),
        in_specs=[smem, smem] + [hbm if k not in (half, half + 1) else pl.BlockSpec(memory_space=pl.ANY) for k in range(parts + 1)] + [vmem] * 4,
        out_specs=vmem,
        out_shape=jax.ShapeDtypeStruct((size * chunk, width if with_base else local), F32 if with_base else BF),
        scratch_shapes=[pltpu.VMEM((size, chunk, width), BF), pltpu.SemaphoreType.DMA((size, parts))],
        compiler_params=pltpu.CompilerParams(vmem_limit_bytes=16 << 20),
        cost_estimate=cost(40 * size * 2 * chunk * width * 4 * local, 3 << 20),
        name="attention",
    )(me, ends, *pieces, *weights, w_out)


def first_join_kernel(context_ref, wo_ref, right_ref, left_ref):
    half = right_ref.shape[0]
    sums = dot(context_ref[...], wo_ref[...]).astype(BF)
    right_ref[...] = sums[:half]
    left_ref[...] = sums[half:]


def join_kernel(at, start, context_ref, wo_ref, recv_ref, out_ref):
    chunk, half = out_ref.shape[0], recv_ref.shape[0]
    sums = dot(context_ref[at * chunk:(at + 1) * chunk], wo_ref[...])
    rows = slice(start, start + half)
    out_ref[rows] = (sums[rows] + recv_ref[...].astype(F32)).astype(BF)
    if half < chunk:
        rest = slice(half - start, chunk - start)
        out_ref[rest] = sums[rest].astype(BF)


def middle_kernel(base_ref, right_ref, left_ref, hidden_ref, normed_ref):
    hidden = base_ref[...] + (right_ref[...].astype(F32) + left_ref[...].astype(F32))
    hidden_ref[...] = hidden
    normed_ref[...] = normalize(hidden).astype(BF)


def feed_kernel(rows_ref, *refs):
    (up_ref, down_ref, gathered_ref, out_ref, ups, downs, sems), hidden = refs[-7:], refs[:-7]
    planes = gathered_ref.shape[1]
    rows = gathered_ref.shape[2] // 2
    copies = [(pltpu.make_async_copy(up_ref, ups.at[0], sems.at[0, 0]),
               pltpu.make_async_copy(down_ref, downs.at[0], sems.at[0, 1]))]
    spread = gathered_ref.shape[0]
    for p in range(planes):
        copies.append(tuple(
            pltpu.make_async_copy(
                gathered_ref.at[:, p, t * rows:(t + 1) * rows, :],
                into.at[p + 1].reshape(spread, rows, into.shape[-1]),
                sems.at[p + 1, t],
            )
            for t, into in enumerate((ups, downs))
        ))
    for up, down in copies:
        up.start()
        down.start()
    normed = rows_ref[...]
    total = hidden[0][...] if hidden else None
    for p, (up, down) in enumerate(copies):
        up.wait()
        inner = jnp.maximum(dot(normed, ups[p]), 0.0).astype(BF)
        down.wait()
        part = dot(inner, downs[p])
        total = part if total is None else total + part
    out_ref[...] = total.astype(out_ref.dtype)


def feed(normed, hidden, w_up, w_down, gathered):
    planes = gathered.shape[1]
    count, width = normed.shape
    vmem = pl.BlockSpec(memory_space=pltpu.VMEM)
    hbm = pl.BlockSpec(memory_space=pltpu.HBM)
    w_up, w_down, gathered = (
        pltpu.with_memory_space_constraint(w, pltpu.HBM) for w in (w_up, w_down, gathered)
    )
    return pl.pallas_call(
        feed_kernel,
        in_specs=[vmem] * (1 + len(hidden)) + [hbm] * 3,
        out_specs=vmem,
        out_shape=jax.ShapeDtypeStruct(normed.shape, F32 if hidden else BF),
        scratch_shapes=[
            pltpu.VMEM((planes + 1,) + w_up.shape, BF),
            pltpu.VMEM((planes + 1,) + w_down.shape, BF),
            pltpu.SemaphoreType.DMA((planes + 1, 2)),
        ],
        compiler_params=pltpu.CompilerParams(vmem_limit_bytes=24 << 20),
        cost_estimate=cost(
            4 * count * width * w_up.shape[1] * (planes + 1), 4 * (planes + 1) * width * w_up.shape[1]
        ),
        name="feed",
    )(normed, *hidden, w_up, w_down, gathered)


def pool_kernel(hidden_ref, pair_ref, gain_ref, member_ref, length_ref, out_ref):
    hidden = hidden_ref[...] + pair_ref[...].astype(F32)
    finished = normalize(hidden) * gain_ref[...]
    pooled = dot(member_ref[...], finished, precision=HIGH) / length_ref[...]
    out_ref[...] = jnp.broadcast_to(pooled[None], out_ref.shape)


def moments_kernel(own, where_ref, pooled_ref, proj_ref, code_ref, out_ref):
    first, core = where_ref[0], where_ref[1]
    parts, few, width = pooled_ref.shape
    sentences = parts * few
    pooled = pooled_ref[...].reshape(sentences, width)
    total = out_ref.shape[0]
    per_chip = width // (total // PACK)
    mean = jnp.mean(pooled, axis=0, keepdims=True)
    large, small = split(pooled - mean)
    feature = lax.broadcasted_iota(jnp.int32, (width, total), 0)
    wanted = lax.broadcasted_iota(jnp.int32, (1, total), 1)
    chosen = jnp.where(wanted % PACK < own, (wanted // PACK) * per_chip + first + wanted % PACK, -1)
    pick = jnp.where(feature == chosen, 1.0, 0.0).astype(BF)
    picked_large, picked_small = dot(large, pick).astype(BF), dot(small, pick).astype(BF)
    rows = ((0,), (0,))
    moments = dot(picked_large, large, rows) + (dot(picked_large, small, rows) + dot(picked_small, large, rows))
    rotated = dot(large, proj_ref[...]).astype(BF)
    lanes = rotated.shape[1]
    chips = total // PACK
    row = lax.broadcasted_iota(jnp.int32, (CORES * KINDS * chips, 1), 0)
    column = lax.broadcasted_iota(jnp.int32, (1, sentences), 1)
    kind = row // chips
    target = ((row % chips) * CORES + core) * KINDS + kind % KINDS
    hit = (target == code_ref[...]) & (column // (sentences // CORES) == kind // KINDS)
    place = jnp.where(hit, 1.0, 0.0)
    there = jnp.broadcast_to(jnp.sum(place, axis=1, keepdims=True), (place.shape[0], lanes))
    wide = [
        jnp.concatenate([part[k * chips:(k + 1) * chips] for k in range(CORES * KINDS)], axis=-1)
        for part in (dot(place.astype(BF), rotated), there)
    ]
    row = lax.broadcasted_iota(jnp.int32, (total, 1), 0)
    column = lax.broadcasted_iota(jnp.int32, (1, CORES * chips), 1)
    spread = (row // PACK == column % chips) & (row % PACK == own + 2 + column // chips)
    sides = dot(jnp.where(spread, 1.0, 0.0).astype(BF), jnp.concatenate(wide, axis=0).astype(BF))
    high = mean.astype(BF).astype(F32)
    low = mean - high
    line = lax.broadcasted_iota(jnp.int32, (total, 1), 0) % PACK
    means = jnp.where(line == own, high, 0.0) + jnp.where(line == own + 1, low, 0.0)
    out_ref[...] = (moments + means + sides).astype(BF)


def combine_kernel(where_ref, recv_ref, proj_ref, pq_ref, cov_ref):
    first = where_ref[0]
    own, width = cov_ref.shape
    recv = recv_ref[...]
    total = recv.shape[0]
    chips = total // PACK
    sentences = pq_ref.shape[1]
    each = float(CORES * sentences)
    row = lax.broadcasted_iota(jnp.int32, (3 * chips + PACK, 1), 0)
    line = lax.broadcasted_iota(jnp.int32, (1, total), 1)
    kind, source = row // chips, row % chips
    away = line - source * PACK
    taken = (kind == 0) & ((away == own) | (away == own + 1))
    taken = taken | ((kind == 1) & (away == own + 2)) | ((kind == 2) & (away == own + 3))
    taken = taken | ((kind == 3) & (line % PACK == source))
    parts = dot(jnp.where(taken, 1.0, 0.0).astype(BF), recv)
    means = parts[:chips]
    sides = parts[chips:2 * chips].astype(BF)
    there = parts[2 * chips:3 * chips].astype(BF)
    within = parts[3 * chips:]
    away = means - jnp.mean(means, axis=0, keepdims=True)
    feature = lax.broadcasted_iota(jnp.int32, (width, LANES), 0)
    lane = lax.broadcasted_iota(jnp.int32, (1, LANES), 1)
    pick = jnp.where(feature == jnp.where(lane < own, first + lane, -1), 1.0, 0.0).astype(BF)
    large, small = split(away)
    picked_large, picked_small = dot(large, pick).astype(BF), dot(small, pick).astype(BF)
    rows = ((0,), (0,))
    between = dot(picked_large, large, rows) + (dot(picked_large, small, rows) + dot(picked_small, large, rows))
    cov_ref[...] = (within[:own] + each * between[:own]) / (each * float(chips))
    shift = dot(large, proj_ref[...]) + dot(small, proj_ref[...])
    shift_large, shift_small = split(shift)
    lanes = shift.shape[1]
    kinds = CORES * KINDS
    stack = lambda wide: jnp.concatenate([wide[:, k * lanes:(k + 1) * lanes] for k in range(kinds)], axis=0)
    size = kinds * chips
    one = lax.broadcasted_iota(jnp.int32, (size, 1), 0)
    other = lax.broadcasted_iota(jnp.int32, (1, size), 1)
    one_kind, one_chip, other_kind, other_chip = one // chips, one % chips, other // chips, other % chips
    ahead = (one_chip < other_chip) | ((one_chip == other_chip) & (one_kind // 2 < other_kind // 2))
    ahead = jnp.where(ahead & (one_kind % 2 == 0), 1.0, 0.0).astype(BF)
    same = jnp.where(one == other, 1.0, 0.0).astype(BF)
    flags = stack(there)[:, :8]
    before = dot(flags, ahead, ((0,), (0,)))[:1]
    here = dot(flags, same, ((0,), (0,)))[:1]
    place = lax.broadcasted_iota(jnp.int32, (sentences, size), 0)
    odd = (lax.broadcasted_iota(jnp.int32, (1, size), 1) // chips) % 2
    position = 2 * before.astype(jnp.int32) + odd
    chosen = jnp.where((place == position) & (here > 0.5), 1.0, 0.0).astype(BF)
    tiled = lambda array: jnp.concatenate([array] * kinds, axis=0)
    result = dot(chosen, stack(sides)) + (dot(chosen, tiled(shift_large)) + dot(chosen, tiled(shift_small)))
    for q in range(pq_ref.shape[0]):
        pq_ref[q] = result[:, q * SUBW:(q + 1) * SUBW]


def small_call(kernel, outs, args, scalar=None, name=None):
    specs = [pl.BlockSpec(memory_space=pltpu.VMEM) for _ in args]
    if scalar is not None:
        specs = [pl.BlockSpec(memory_space=pltpu.SMEM)] + specs
        args = (scalar,) + tuple(args)
    single = not isinstance(outs, (tuple, list))
    return pl.pallas_call(
        kernel,
        in_specs=specs,
        out_specs=pl.BlockSpec(memory_space=pltpu.VMEM) if single else [pl.BlockSpec(memory_space=pltpu.VMEM) for _ in outs],
        out_shape=outs,
        compiler_params=pltpu.CompilerParams(vmem_limit_bytes=16 << 20),
        cost_estimate=cost(1 << 20, 1 << 20),
        name=name,
    )(*args)


def on_device(
    tokens, lengths, dest, w_query, w_key, w_value, w_out, w_up, w_down, final_gain, projection
):
    dp_count = lax.axis_size("dp")
    sub_count = lax.axis_size("sub")
    dp_at = lax.axis_index("dp")
    sub_at = lax.axis_index("sub")
    block_count, per_block = lengths.shape
    local_rows, local_width = tokens.shape
    block_rows = local_rows // block_count
    width = local_width * sub_count
    own_blocks = block_count // sub_count
    own_rows = own_blocks * block_rows
    half = sub_count // 2

    def move(array, by):
        return lax.ppermute(array, "sub", [(i, (i + by) % sub_count) for i in range(sub_count)])

    def swap(array):
        return lax.ppermute(array, "sub", [(i, i ^ 1) for i in range(sub_count)])

    rows = w_up.shape[0] // dp_count
    piece = jnp.concatenate(
        [lax.dynamic_slice_in_dim(w, dp_at * rows, rows, 0) for w in (w_up, w_down)], axis=0
    )
    across = lax.ppermute(
        piece, "sub", [(i, (i + (half - 1 if i % 2 else 1 - half)) % sub_count) for i in range(sub_count)]
    )
    others = [move(piece, 2), move(piece, -2), across]
    planes = len(others)

    ends = jnp.cumsum(lengths, axis=-1)
    position = jnp.arange(block_rows, dtype=jnp.int32)
    segment = jnp.sum((ends[:, None, :] <= position[None, :, None]).astype(jnp.int32), axis=-1)
    ordinal = jnp.arange(block_count, dtype=jnp.int32)
    keys = (ordinal[:, None] * per_block + segment).reshape(local_rows)
    own_lens = lax.dynamic_slice_in_dim(lengths, sub_at * own_blocks, own_blocks, 0)
    own_keys = lax.dynamic_slice_in_dim(keys, sub_at * own_rows, own_rows, 0)
    own_sentences = own_blocks * per_block
    member = (
        own_keys[None, :] == sub_at * own_sentences + jnp.arange(own_sentences, dtype=jnp.int32)[:, None]
    ).astype(F32)
    matches = dest[:, None] == dest[None, :]
    earlier = ordinal[:, None] > ordinal[None, :]
    earlier_count = jnp.sum((matches & earlier).astype(jnp.int32), axis=1)
    code = (dest * SLOTS + earlier_count)[:, None] * per_block + jnp.arange(per_block, dtype=jnp.int32)[None, :]
    code = code.reshape(1, block_count * per_block)
    chips = dp_count // CORES
    siblings = [[q * CORES + c for c in range(CORES)] for q in range(chips)]
    other = lax.ppermute(code, "dp", [(i, i ^ 1) for i in range(dp_count)])
    core = dp_at % CORES
    code = jnp.where(core == 0, jnp.concatenate((code, other), axis=1), jnp.concatenate((other, code), axis=1))
    columns = width // sub_count
    proj = lax.dynamic_slice_in_dim(projection, sub_at * columns, columns, 1)

    behind, ahead = [], []
    right = left = tokens
    for step in range(half - 1):
        right, left = move(right, 1), move(left, -1)
        if step == 0:
            others = lax.optimization_barrier((others, right, left))[0]
        behind.append(right)
        ahead.append(left)
    halfway = local_rows // 2
    far = [move(right[:halfway], 1), move(left[halfway:], -1)]
    pieces = [tokens] + ahead + far + behind

    gathered = lax.all_gather(jnp.concatenate(others, axis=0), "dp", axis=0, tiled=True)
    gathered = gathered.reshape(dp_count, planes, 2 * rows, width)

    attend = functools.partial(attention, pieces, (w_query, w_key, w_value), w_out, lengths.T, sub_at.reshape(1))
    own_shape = (own_rows, width)
    half_shape = (own_rows // 2, width)
    right, left = small_call(
        first_join_kernel,
        [jax.ShapeDtypeStruct(half_shape, BF)] * 2,
        (attend([half]), w_out),
        name="join",
    )
    right, left = move(right, 1), move(left, -1)
    for away in range(half - 1, 0, -1):
        context = attend([away, -away])
        join = lambda at, start, recv: small_call(
            functools.partial(join_kernel, at, start),
            jax.ShapeDtypeStruct(own_shape, BF),
            (context, w_out, recv),
            name="join",
        )
        right, left = move(join(0, 0, right), 1), move(join(1, own_rows - left.shape[0], left), -1)
    base = attend([0], with_base=True)
    hidden1, normed2 = small_call(
        middle_kernel,
        (jax.ShapeDtypeStruct(own_shape, F32), jax.ShapeDtypeStruct(own_shape, BF)),
        (base, right, left),
        name="middle",
    )
    sent = feed(swap(normed2), (), w_up, w_down, gathered)
    hidden2 = feed(normed2, (hidden1,), w_up, w_down, gathered)
    pooled = small_call(
        pool_kernel,
        jax.ShapeDtypeStruct((sub_count, own_sentences, width), F32),
        (hidden2, swap(sent), final_gain[None, :], member, own_lens.reshape(own_sentences, 1).astype(F32)),
        name="pool",
    )
    pooled = lax.all_to_all(pooled, "sub", split_axis=0, concat_axis=0, tiled=True)
    pooled = lax.all_gather(pooled, "dp", axis=0, tiled=True, axis_index_groups=siblings)
    sentences = sub_count * own_sentences
    cov_rows = width // (dp_count * sub_count)
    sent = small_call(
        functools.partial(moments_kernel, cov_rows),
        jax.ShapeDtypeStruct((chips * PACK, width), BF),
        (pooled, proj, code),
        scalar=jnp.stack([(core * sub_count + sub_at) * cov_rows, core]).astype(jnp.int32),
        name="moments",
    )
    received = lax.all_to_all(
        sent.reshape(chips, PACK, width), "dp", split_axis=0, concat_axis=0, tiled=True,
        axis_index_groups=[[q * CORES + c for q in range(chips)] for c in range(CORES)],
    ).reshape(chips * PACK, width)
    return small_call(
        combine_kernel,
        (
            jax.ShapeDtypeStruct((columns // SUBW, sentences, SUBW), F32),
            jax.ShapeDtypeStruct((cov_rows, width), F32),
        ),
        (received, proj),
        scalar=((dp_at * sub_count + sub_at) * cov_rows).reshape(1),
        name="combine",
    )


def solution(mesh):
    in_specs = (
        P("dp", "sub"),
        P("dp", None),
        P("dp"),
        P(None, "sub"),
        P(None, "sub"),
        P(None, "sub"),
        P("sub", None),
        P(None, "sub"),
        P("sub", None),
        P(),
        P(),
    )
    out_specs = (P("sub", "dp", None), P(("dp", "sub"), None))
    return jax.shard_map(
        on_device, mesh=mesh, in_specs=in_specs, out_specs=out_specs, check_vma=False
    )
```

```python
import functools
import math

import jax
import jax.numpy as jnp
from jax import lax
from jax.experimental import pallas as pl
from jax.experimental.pallas import tpu as pltpu
from jax.sharding import PartitionSpec as P

HDIM = 64
SUBW = 64
LANES = 128
SLOTS = 2
CORES = 2
KINDS = 4
PACK = 8

epsilon = 1e-05
BF = jnp.bfloat16
F32 = jnp.float32
HIGH = lax.Precision.HIGHEST


def normalize(rows):
    center = jnp.mean(rows, axis=-1, keepdims=True)
    shifted = rows - center
    spread = jnp.mean(shifted * shifted, axis=-1, keepdims=True)
    return shifted * lax.rsqrt(spread + epsilon)


def dot(a, b, dims=((1,), (0,)), precision=None):
    return lax.dot_general(a, b, (dims, ((), ())), precision=precision, preferred_element_type=F32)


def split(array):
    high = array.astype(BF)
    return high, (array - high.astype(F32)).astype(BF)


def cost(flops, size):
    return pl.CostEstimate(flops=flops, bytes_accessed=size, transcendentals=0)


def attention_kernel(offsets, parts, chunk, with_base, me_ref, ends_ref, *refs):
    pieces, (wq_ref, wk_ref, wv_ref, wo_ref), rest = refs[:parts + 1], refs[parts + 1:parts + 5], refs[parts + 5:]
    out_ref, rows_ref, sems = rest
    me = me_ref[0]
    half = parts // 2
    part = pieces[0].shape[1]
    chunks = [lax.rem(me + (off + parts), parts) for off in offsets]

    def slot(i, away):
        at = lax.rem(me + (away + parts), parts)
        return rows_ref.at[i, :, pl.ds(pl.multiple_of(at * part, part), part)]

    def fetch(source, start, i, away, number):
        start = pl.multiple_of(start, chunk)
        return pltpu.make_async_copy(source.at[pl.ds(start, chunk), :], slot(i, away), sems.at[i, number])

    for i, c in enumerate(chunks):
        for k in range(half):
            fetch(pieces[k], c * chunk, i, k, k).start()
        for k in range(1, half):
            fetch(pieces[half + 1 + k], c * chunk, i, -k, half + k).start()

        @pl.when(c < half)
        def _():
            fetch(pieces[half], c * chunk, i, half, half).start()

        @pl.when(c >= half)
        def _():
            fetch(pieces[half + 1], (c - half) * chunk, i, half, half).start()

    for i, c in enumerate(chunks):
        for k in range(half):
            fetch(pieces[k], c * chunk, i, k, k).wait()
        for k in range(1, half):
            fetch(pieces[half + 1 + k], c * chunk, i, -k, half + k).wait()
        fetch(pieces[half], 0, i, half, half).wait()
    count = len(offsets)
    rows = rows_ref[...].reshape(count * chunk, -1).astype(F32)
    normed = normalize(rows).astype(BF)
    w_qkv = jnp.concatenate([wq_ref[...], wk_ref[...], wv_ref[...]], axis=1)
    projected = dot(normed, w_qkv).astype(BF)
    local = wo_ref.shape[0]
    block_rows = chunk * parts // ends_ref.shape[1]
    blocks = chunk // block_rows
    per_block = ends_ref.shape[0]

    def keys(c, shape, axis):
        row = lax.broadcasted_iota(jnp.int32, shape, axis)
        block = row // block_rows
        key = block * per_block
        for b in range(blocks):
            end = b * block_rows
            for e in range(per_block - 1):
                end = end + ends_ref[e, c * blocks + b]
                key = key + jnp.where((block == b) & (row >= end), 1, 0)
        return key

    lines = []
    for i, c in enumerate(chunks):
        mine = projected[i * chunk:(i + 1) * chunk]
        matches = keys(c, (chunk, 1), 0) == keys(c, (1, chunk), 1)
        heads = []
        for h in range(local // HDIM):
            query, key, value = (
                mine[:, t * local + h * HDIM:t * local + (h + 1) * HDIM] for t in range(3)
            )
            scores = dot(query, key, ((1,), (1,))) / math.sqrt(HDIM)
            raised = jnp.where(matches, jnp.exp(scores), 0.0)
            weights = (raised / jnp.sum(raised, axis=-1, keepdims=True)).astype(BF)
            heads.append(dot(weights, value).astype(BF))
        lines.append(jnp.concatenate(heads, axis=-1))
    context = jnp.concatenate(lines, axis=0)
    if with_base:
        out_ref[...] = rows + dot(context, wo_ref[...])
    else:
        out_ref[...] = context


def attention(pieces, weights, w_out, ends, me, offsets, with_base=False):
    parts = len(pieces) - 1
    count, part = pieces[0].shape
    chunk = count // parts
    local, width = w_out.shape
    size = len(offsets)
    smem = pl.BlockSpec(memory_space=pltpu.SMEM)
    vmem = pl.BlockSpec(memory_space=pltpu.VMEM)
    hbm = pl.BlockSpec(memory_space=pltpu.HBM)
    half = parts // 2
    pieces = [
        p if k in (half, half + 1) else pltpu.with_memory_space_constraint(p, pltpu.HBM) for k, p in enumerate(pieces)
    ]
    return pl.pallas_call(
        functools.partial(attention_kernel, offsets, parts, chunk, with_base),
        in_specs=[smem, smem] + [hbm if k not in (half, half + 1) else pl.BlockSpec(memory_space=pl.ANY) for k in range(parts + 1)] + [vmem] * 4,
        out_specs=vmem,
        out_shape=jax.ShapeDtypeStruct((size * chunk, width if with_base else local), F32 if with_base else BF),
        scratch_shapes=[pltpu.VMEM((size, chunk, width), BF), pltpu.SemaphoreType.DMA((size, parts))],
        compiler_params=pltpu.CompilerParams(vmem_limit_bytes=16 << 20),
        cost_estimate=cost(40 * size * 2 * chunk * width * 4 * local, 3 << 20),
        name="attention",
    )(me, ends, *pieces, *weights, w_out)


def first_join_kernel(context_ref, wo_ref, right_ref, left_ref):
    half = right_ref.shape[0]
    sums = dot(context_ref[...], wo_ref[...]).astype(BF)
    right_ref[...] = sums[:half]
    left_ref[...] = sums[half:]


def join_kernel(at, start, context_ref, wo_ref, recv_ref, out_ref):
    chunk, half = out_ref.shape[0], recv_ref.shape[0]
    sums = dot(context_ref[at * chunk:(at + 1) * chunk], wo_ref[...])
    rows = slice(start, start + half)
    out_ref[rows] = (sums[rows] + recv_ref[...].astype(F32)).astype(BF)
    if half < chunk:
        rest = slice(half - start, chunk - start)
        out_ref[rest] = sums[rest].astype(BF)


def middle_kernel(base_ref, right_ref, left_ref, hidden_ref, normed_ref):
    hidden = base_ref[...] + (right_ref[...].astype(F32) + left_ref[...].astype(F32))
    hidden_ref[...] = hidden
    normed_ref[...] = normalize(hidden).astype(BF)


def feed_kernel(rows_ref, *refs):
    (up_ref, down_ref, gathered_ref, out_ref, ups, downs, sems), hidden = refs[-7:], refs[:-7]
    planes = gathered_ref.shape[1]
    rows = gathered_ref.shape[2] // 2
    copies = [(pltpu.make_async_copy(up_ref, ups.at[0], sems.at[0, 0]),
               pltpu.make_async_copy(down_ref, downs.at[0], sems.at[0, 1]))]
    spread = gathered_ref.shape[0]
    for p in range(planes):
        copies.append(tuple(
            pltpu.make_async_copy(
                gathered_ref.at[:, p, t * rows:(t + 1) * rows, :],
                into.at[p + 1].reshape(spread, rows, into.shape[-1]),
                sems.at[p + 1, t],
            )
            for t, into in enumerate((ups, downs))
        ))
    for up, down in copies:
        up.start()
        down.start()
    normed = rows_ref[...]
    total = hidden[0][...] if hidden else None
    for p, (up, down) in enumerate(copies):
        up.wait()
        inner = jnp.maximum(dot(normed, ups[p]), 0.0).astype(BF)
        down.wait()
        part = dot(inner, downs[p])
        total = part if total is None else total + part
    out_ref[...] = total.astype(out_ref.dtype)


def feed(normed, hidden, w_up, w_down, gathered):
    planes = gathered.shape[1]
    count, width = normed.shape
    vmem = pl.BlockSpec(memory_space=pltpu.VMEM)
    hbm = pl.BlockSpec(memory_space=pltpu.HBM)
    w_up, w_down, gathered = (
        pltpu.with_memory_space_constraint(w, pltpu.HBM) for w in (w_up, w_down, gathered)
    )
    return pl.pallas_call(
        feed_kernel,
        in_specs=[vmem] * (1 + len(hidden)) + [hbm] * 3,
        out_specs=vmem,
        out_shape=jax.ShapeDtypeStruct(normed.shape, F32 if hidden else BF),
        scratch_shapes=[
            pltpu.VMEM((planes + 1,) + w_up.shape, BF),
            pltpu.VMEM((planes + 1,) + w_down.shape, BF),
            pltpu.SemaphoreType.DMA((planes + 1, 2)),
        ],
        compiler_params=pltpu.CompilerParams(vmem_limit_bytes=24 << 20),
        cost_estimate=cost(
            4 * count * width * w_up.shape[1] * (planes + 1), 4 * (planes + 1) * width * w_up.shape[1]
        ),
        name="feed",
    )(normed, *hidden, w_up, w_down, gathered)


def pool_kernel(hidden_ref, pair_ref, gain_ref, member_ref, length_ref, out_ref):
    hidden = hidden_ref[...] + pair_ref[...].astype(F32)
    finished = normalize(hidden) * gain_ref[...]
    pooled = dot(member_ref[...], finished, precision=HIGH) / length_ref[...]
    out_ref[...] = jnp.broadcast_to(pooled[None], out_ref.shape)


def moments_kernel(own, where_ref, pooled_ref, proj_ref, code_ref, out_ref):
    first, core = where_ref[0], where_ref[1]
    parts, few, width = pooled_ref.shape
    sentences = parts * few
    pooled = pooled_ref[...].reshape(sentences, width)
    total = out_ref.shape[0]
    per_chip = width // (total // PACK)
    mean = jnp.mean(pooled, axis=0, keepdims=True)
    large, small = split(pooled - mean)
    feature = lax.broadcasted_iota(jnp.int32, (width, total), 0)
    wanted = lax.broadcasted_iota(jnp.int32, (1, total), 1)
    chosen = jnp.where(wanted % PACK < own, (wanted // PACK) * per_chip + first + wanted % PACK, -1)
    pick = jnp.where(feature == chosen, 1.0, 0.0).astype(BF)
    picked_large, picked_small = dot(large, pick).astype(BF), dot(small, pick).astype(BF)
    rows = ((0,), (0,))
    moments = dot(picked_large, large, rows) + (dot(picked_large, small, rows) + dot(picked_small, large, rows))
    rotated = dot(large, proj_ref[...]).astype(BF)
    lanes = rotated.shape[1]
    chips = total // PACK
    row = lax.broadcasted_iota(jnp.int32, (CORES * KINDS * chips, 1), 0)
    column = lax.broadcasted_iota(jnp.int32, (1, sentences), 1)
    kind = row // chips
    target = ((row % chips) * CORES + core) * KINDS + kind % KINDS
    hit = (target == code_ref[...]) & (column // (sentences // CORES) == kind // KINDS)
    place = jnp.where(hit, 1.0, 0.0)
    there = jnp.broadcast_to(jnp.sum(place, axis=1, keepdims=True), (place.shape[0], lanes))
    wide = [
        jnp.concatenate([part[k * chips:(k + 1) * chips] for k in range(CORES * KINDS)], axis=-1)
        for part in (dot(place.astype(BF), rotated), there)
    ]
    row = lax.broadcasted_iota(jnp.int32, (total, 1), 0)
    column = lax.broadcasted_iota(jnp.int32, (1, CORES * chips), 1)
    spread = (row // PACK == column % chips) & (row % PACK == own + 2 + column // chips)
    sides = dot(jnp.where(spread, 1.0, 0.0).astype(BF), jnp.concatenate(wide, axis=0).astype(BF))
    high = mean.astype(BF).astype(F32)
    low = mean - high
    line = lax.broadcasted_iota(jnp.int32, (total, 1), 0) % PACK
    means = jnp.where(line == own, high, 0.0) + jnp.where(line == own + 1, low, 0.0)
    out_ref[...] = (moments + means + sides).astype(BF)


def combine_kernel(where_ref, recv_ref, proj_ref, pq_ref, cov_ref):
    first = where_ref[0]
    own, width = cov_ref.shape
    recv = recv_ref[...]
    total = recv.shape[0]
    chips = total // PACK
    sentences = pq_ref.shape[1]
    each = float(CORES * sentences)
    row = lax.broadcasted_iota(jnp.int32, (3 * chips + PACK, 1), 0)
    line = lax.broadcasted_iota(jnp.int32, (1, total), 1)
    kind, source = row // chips, row % chips
    away = line - source * PACK
    taken = (kind == 0) & ((away == own) | (away == own + 1))
    taken = taken | ((kind == 1) & (away == own + 2)) | ((kind == 2) & (away == own + 3))
    taken = taken | ((kind == 3) & (line % PACK == source))
    parts = dot(jnp.where(taken, 1.0, 0.0).astype(BF), recv)
    means = parts[:chips]
    sides = parts[chips:2 * chips].astype(BF)
    there = parts[2 * chips:3 * chips].astype(BF)
    within = parts[3 * chips:]
    away = means - jnp.mean(means, axis=0, keepdims=True)
    feature = lax.broadcasted_iota(jnp.int32, (width, LANES), 0)
    lane = lax.broadcasted_iota(jnp.int32, (1, LANES), 1)
    pick = jnp.where(feature == jnp.where(lane < own, first + lane, -1), 1.0, 0.0).astype(BF)
    large, small = split(away)
    picked_large, picked_small = dot(large, pick).astype(BF), dot(small, pick).astype(BF)
    rows = ((0,), (0,))
    between = dot(picked_large, large, rows) + (dot(picked_large, small, rows) + dot(picked_small, large, rows))
    cov_ref[...] = (within[:own] + each * between[:own]) / (each * float(chips))
    shift = dot(large, proj_ref[...]) + dot(small, proj_ref[...])
    shift_large, shift_small = split(shift)
    lanes = shift.shape[1]
    kinds = CORES * KINDS
    stack = lambda wide: jnp.concatenate([wide[:, k * lanes:(k + 1) * lanes] for k in range(kinds)], axis=0)
    size = kinds * chips
    one = lax.broadcasted_iota(jnp.int32, (size, 1), 0)
    other = lax.broadcasted_iota(jnp.int32, (1, size), 1)
    one_kind, one_chip, other_kind, other_chip = one // chips, one % chips, other // chips, other % chips
    ahead = (one_chip < other_chip) | ((one_chip == other_chip) & (one_kind // 2 < other_kind // 2))
    ahead = jnp.where(ahead & (one_kind % 2 == 0), 1.0, 0.0).astype(BF)
    same = jnp.where(one == other, 1.0, 0.0).astype(BF)
    flags = stack(there)[:, :8]
    before = dot(flags, ahead, ((0,), (0,)))[:1]
    here = dot(flags, same, ((0,), (0,)))[:1]
    place = lax.broadcasted_iota(jnp.int32, (sentences, size), 0)
    odd = (lax.broadcasted_iota(jnp.int32, (1, size), 1) // chips) % 2
    position = 2 * before.astype(jnp.int32) + odd
    chosen = jnp.where((place == position) & (here > 0.5), 1.0, 0.0).astype(BF)
    tiled = lambda array: jnp.concatenate([array] * kinds, axis=0)
    result = dot(chosen, stack(sides)) + (dot(chosen, tiled(shift_large)) + dot(chosen, tiled(shift_small)))
    for q in range(pq_ref.shape[0]):
        pq_ref[q] = result[:, q * SUBW:(q + 1) * SUBW]


def small_call(kernel, outs, args, scalar=None, name=None):
    specs = [pl.BlockSpec(memory_space=pltpu.VMEM) for _ in args]
    if scalar is not None:
        specs = [pl.BlockSpec(memory_space=pltpu.SMEM)] + specs
        args = (scalar,) + tuple(args)
    single = not isinstance(outs, (tuple, list))
    return pl.pallas_call(
        kernel,
        in_specs=specs,
        out_specs=pl.BlockSpec(memory_space=pltpu.VMEM) if single else [pl.BlockSpec(memory_space=pltpu.VMEM) for _ in outs],
        out_shape=outs,
        compiler_params=pltpu.CompilerParams(vmem_limit_bytes=16 << 20),
        cost_estimate=cost(1 << 20, 1 << 20),
        name=name,
    )(*args)


def on_device(
    tokens, lengths, dest, w_query, w_key, w_value, w_out, w_up, w_down, final_gain, projection
):
    dp_count = lax.axis_size("dp")
    sub_count = lax.axis_size("sub")
    dp_at = lax.axis_index("dp")
    sub_at = lax.axis_index("sub")
    block_count, per_block = lengths.shape
    local_rows, local_width = tokens.shape
    block_rows = local_rows // block_count
    width = local_width * sub_count
    own_blocks = block_count // sub_count
    own_rows = own_blocks * block_rows
    half = sub_count // 2

    def move(array, by):
        return lax.ppermute(array, "sub", [(i, (i + by) % sub_count) for i in range(sub_count)])

    def swap(array):
        return lax.ppermute(array, "sub", [(i, i ^ 1) for i in range(sub_count)])

    rows = w_up.shape[0] // dp_count
    piece = jnp.concatenate(
        [lax.dynamic_slice_in_dim(w, dp_at * rows, rows, 0) for w in (w_up, w_down)], axis=0
    )
    across = lax.ppermute(
        piece, "sub", [(i, (i + (half - 1 if i % 2 else 1 - half)) % sub_count) for i in range(sub_count)]
    )
    others = [move(piece, 2), move(piece, -2), across]
    planes = len(others)

    ends = jnp.cumsum(lengths, axis=-1)
    position = jnp.arange(block_rows, dtype=jnp.int32)
    segment = jnp.sum((ends[:, None, :] <= position[None, :, None]).astype(jnp.int32), axis=-1)
    ordinal = jnp.arange(block_count, dtype=jnp.int32)
    keys = (ordinal[:, None] * per_block + segment).reshape(local_rows)
    own_lens = lax.dynamic_slice_in_dim(lengths, sub_at * own_blocks, own_blocks, 0)
    own_keys = lax.dynamic_slice_in_dim(keys, sub_at * own_rows, own_rows, 0)
    own_sentences = own_blocks * per_block
    member = (
        own_keys[None, :] == sub_at * own_sentences + jnp.arange(own_sentences, dtype=jnp.int32)[:, None]
    ).astype(F32)
    matches = dest[:, None] == dest[None, :]
    earlier = ordinal[:, None] > ordinal[None, :]
    earlier_count = jnp.sum((matches & earlier).astype(jnp.int32), axis=1)
    code = (dest * SLOTS + earlier_count)[:, None] * per_block + jnp.arange(per_block, dtype=jnp.int32)[None, :]
    code = code.reshape(1, block_count * per_block)
    chips = dp_count // CORES
    siblings = [[q * CORES + c for c in range(CORES)] for q in range(chips)]
    other = lax.ppermute(code, "dp", [(i, i ^ 1) for i in range(dp_count)])
    core = dp_at % CORES
    code = jnp.where(core == 0, jnp.concatenate((code, other), axis=1), jnp.concatenate((other, code), axis=1))
    columns = width // sub_count
    proj = lax.dynamic_slice_in_dim(projection, sub_at * columns, columns, 1)

    behind, ahead = [], []
    right = left = tokens
    for step in range(half - 1):
        right, left = move(right, 1), move(left, -1)
        if step == 0:
            others = lax.optimization_barrier((others, right, left))[0]
        behind.append(right)
        ahead.append(left)
    halfway = local_rows // 2
    far = [move(right[:halfway], 1), move(left[halfway:], -1)]
    pieces = [tokens] + ahead + far + behind

    gathered = lax.all_gather(jnp.concatenate(others, axis=0), "dp", axis=0, tiled=True)
    gathered = gathered.reshape(dp_count, planes, 2 * rows, width)

    attend = functools.partial(attention, pieces, (w_query, w_key, w_value), w_out, lengths.T, sub_at.reshape(1))
    own_shape = (own_rows, width)
    half_shape = (own_rows // 2, width)
    right, left = small_call(
        first_join_kernel,
        [jax.ShapeDtypeStruct(half_shape, BF)] * 2,
        (attend([half]), w_out),
        name="join",
    )
    left, right = move(left, -1), move(right, 1)
    for away in range(half - 1, 0, -1):
        context = attend([-away, away])
        join = lambda at, start, recv: small_call(
            functools.partial(join_kernel, at, start),
            jax.ShapeDtypeStruct(own_shape, BF),
            (context, w_out, recv),
            name="join",
        )
        left = move(join(0, own_rows - left.shape[0], left), -1)
        right = move(join(1, 0, right), 1)
    base = attend([0], with_base=True)
    hidden1, normed2 = small_call(
        middle_kernel,
        (jax.ShapeDtypeStruct(own_shape, F32), jax.ShapeDtypeStruct(own_shape, BF)),
        (base, right, left),
        name="middle",
    )
    sent = feed(swap(normed2), (), w_up, w_down, gathered)
    hidden2 = feed(normed2, (hidden1,), w_up, w_down, gathered)
    pooled = small_call(
        pool_kernel,
        jax.ShapeDtypeStruct((sub_count, own_sentences, width), F32),
        (hidden2, swap(sent), final_gain[None, :], member, own_lens.reshape(own_sentences, 1).astype(F32)),
        name="pool",
    )
    pooled = lax.all_to_all(pooled, "sub", split_axis=0, concat_axis=0, tiled=True)
    pooled = lax.all_gather(pooled, "dp", axis=0, tiled=True, axis_index_groups=siblings)
    sentences = sub_count * own_sentences
    cov_rows = width // (dp_count * sub_count)
    sent = small_call(
        functools.partial(moments_kernel, cov_rows),
        jax.ShapeDtypeStruct((chips * PACK, width), BF),
        (pooled, proj, code),
        scalar=jnp.stack([(core * sub_count + sub_at) * cov_rows, core]).astype(jnp.int32),
        name="moments",
    )
    received = lax.all_to_all(
        sent.reshape(chips, PACK, width), "dp", split_axis=0, concat_axis=0, tiled=True,
        axis_index_groups=[[q * CORES + c for q in range(chips)] for c in range(CORES)],
    ).reshape(chips * PACK, width)
    return small_call(
        combine_kernel,
        (
            jax.ShapeDtypeStruct((columns // SUBW, sentences, SUBW), F32),
            jax.ShapeDtypeStruct((cov_rows, width), F32),
        ),
        (received, proj),
        scalar=((dp_at * sub_count + sub_at) * cov_rows).reshape(1),
        name="combine",
    )


def solution(mesh):
    in_specs = (
        P("dp", "sub"),
        P("dp", None),
        P("dp"),
        P(None, "sub"),
        P(None, "sub"),
        P(None, "sub"),
        P("sub", None),
        P(None, "sub"),
        P("sub", None),
        P(),
        P(),
    )
    out_specs = (P("sub", "dp", None), P(("dp", "sub"), None))
    return jax.shard_map(
        on_device, mesh=mesh, in_specs=in_specs, out_specs=out_specs, check_vma=False
    )
```
